128 devices in a mesh: slab: 4 (over z), ang: 32 (over x, y, core).
Axes of the slice: x: 4, y: 4, z: 4, core: 2. Of those that a mesh axis runs over, the one named last changes fastest.
Arguments:
- object_slices: float32 [2, 1024, 128, 128], P(None, ('slab', 'ang')), may hold values from -6 to 6
- views: float32 [2, 1024, 32, 128], P(None, 'slab', 'ang'), may hold values from -6 to 6
- scaled_dual: float32 [2, 1024, 32, 128], P(None, 'slab', 'ang'), may hold values from -6 to 6
- probe: float32 [2, 128, 128], replicated, may hold values from -3 to 3
- intensities: bfloat16 [32, 48, 128, 128], P('ang', 'slab'), may hold values from 0 to 2
- tile_rows: int32 [32, 48], P('ang', 'slab'), may hold values from 0 to 15
- live_counts: int32 [32, 4], P('ang', 'slab'), may hold values from 1 to 12, as said below
Outputs:
- object_new: float32 [2, 1024, 128, 128], P(None, ('slab', 'ang'))
- views_new: float32 [2, 1024, 32, 128], P(None, 'slab', 'ang')
- dual_new: float32 [2, 1024, 32, 128], P(None, 'slab', 'ang')
- probe_new: float32 [2, 128, 128], replicated
The draws below stay inside these ranges and needn't reach their ends.
Inputs may be any that keep to these rules, and one draw needn't show every extreme that they name: `tile_rows`: a slot's patch starts 16 times this value rows into its slab and may reach 112 rows into the next slab. `live_counts`: slots at and past the count of their angle and slab carry no data; some angle and slab have all 12 slots live.
All inputs are finite; a program needn't handle non-finite values.
Results may differ from the reference program's by a relative error of at most 0.0028.
The reference program's roundings to bfloat16 on the way count: a program that leaves them out, or rounds other values in their place, can miss the bound.
Values sent between devices are 32-bit elements; how exact they have to be, the bound alone decides.
A program may use at most 64 MiB of HBM per device.

```python
import math
import jax
import jax.numpy as jnp
from jax import lax

PROBE = 128
WIDTH = 128
STEP = 16
SLAB_ROWS = 256
CAP = 12
TILES = 16
ANGLES = 32
SLICES = 1024
SLICE_DEV = 8
N_SLAB = 4


def draw_live_counts(key, part):
    key = jax.random.fold_in(key, 11)
    key_base, key_heavy, key_pick = jax.random.split(key, 3)
    base = jax.random.randint(key_base, (ANGLES, N_SLAB), 1, CAP // 2 + 1)
    heavy = jax.random.randint(key_heavy, (ANGLES, N_SLAB), 0, 4) == 0
    picked = jax.random.randint(key_pick, (), 0, ANGLES * N_SLAB)
    position = jnp.arange(ANGLES * N_SLAB, dtype=jnp.int32).reshape(ANGLES, N_SLAB)
    full = jnp.logical_or(heavy, position == picked)
    return jnp.where(full, CAP, base).astype(jnp.int32)


def set_ends(values, rng, low, top_value):
    shape = values.shape
    spot = [jax.random.randint(jax.random.fold_in(rng, axis), (), 0, shape[axis]) for axis in range(len(shape))]
    values = values.at[tuple(spot)].set(low)
    longest = shape.index(max(shape))
    spot[longest] = (spot[longest] + 1) % shape[longest]
    return values.at[tuple(spot)].set(top_value)


def block_scale(rng, extent, cuts, low, largest):
    def one(dim, blocks):
        heights = jax.random.uniform(jax.random.fold_in(jax.random.fold_in(rng, 6), dim), (blocks,), jnp.float32, low / len(cuts), largest / len(cuts))
        return jnp.repeat(jnp.exp(heights), extent[dim] // blocks).reshape((-1,) + (1,) * (len(extent) - dim - 1))

    factor_of = one(*cuts[0])
    for cut in cuts[1:]:
        factor_of = factor_of * one(*cut)
    return factor_of


def scatter_about(own_key, dims, scale, reach, cuts=(), kind=jnp.bfloat16):
    values = scale * jax.random.normal(own_key, dims, jnp.float32)
    if cuts:
        values = values * block_scale(own_key, dims, cuts, -0.22, 0.18)
    return jnp.clip(values, -reach, reach).astype(kind)


def setup_inputs(seed: int = 0) -> dict:
    key_list = jax.random.split(jax.random.key(seed), 8)
    object_slices = scatter_about(key_list[0], (2, SLICES, WIDTH, WIDTH), 1.0, 6.0, ((1, 128),), jnp.float32)
    views = scatter_about(key_list[1], (2, SLICES, ANGLES, WIDTH), 1.0, 6.0, ((1, 4), (2, 32)), jnp.float32)
    scaled_dual = scatter_about(key_list[2], (2, SLICES, ANGLES, WIDTH), 1.0, 6.0, ((1, 4), (2, 32)), jnp.float32)
    probe = scatter_about(key_list[3], (2, PROBE, PROBE), 0.5, 3.0, (), jnp.float32)
    intensities = jnp.clip(2.0 * jax.random.uniform(key_list[4], (ANGLES, N_SLAB * CAP, PROBE, PROBE), jnp.float32) ** block_scale(key_list[4], (ANGLES, N_SLAB * CAP, PROBE, PROBE), ((0, 32), (1, 4)), -0.2, 0.2), 0.0, 2.0).astype(jnp.bfloat16)
    tile_rows = set_ends(jax.random.randint(key_list[5], (ANGLES, N_SLAB * CAP), 0, TILES), jax.random.fold_in(key_list[5], 1), 0, TILES - 1).astype(jnp.int32)
    live_counts = draw_live_counts(jax.random.fold_in(key_list[7], 71), 0)
    return {"object_slices": object_slices, "views": views, "scaled_dual": scaled_dual, "probe": probe, "intensities": intensities, "tile_rows": tile_rows, "live_counts": live_counts}


view_rate = 0.1
penalty = 1.0
probe_rate = 16.0
epsilon = 1e-06

def dft_tables(length):
    counter = jnp.arange(length, dtype=jnp.int32)
    product = counter[:, None] * counter[None, :] % length
    angle_table = product.astype(jnp.float32) * (2.0 * math.pi / length)
    factor = 1.0 / math.sqrt(length)
    return (jnp.cos(angle_table) * factor, jnp.sin(angle_table) * factor)

def parity_sign(length):
    counter = jnp.arange(length, dtype=jnp.int32)
    return (1 - 2 * (counter % 2)).astype(jnp.float32)

def axis_factor(along, length):
    floor_v = jnp.floor(along)
    frac = along - floor_v
    base = floor_v.astype(jnp.int32)
    cells = jnp.arange(length, dtype=jnp.int32)
    lower = (cells[None, None, :] == (base % length)[:, :, None]).astype(jnp.float32)
    upper = (cells[None, None, :] == ((base + 1) % length)[:, :, None]).astype(jnp.float32)
    return (1.0 - frac)[:, :, None] * lower + frac[:, :, None] * upper

def line_factors(angle_count, length):
    turns = jnp.arange(angle_count, dtype=jnp.int32).astype(jnp.float32) * (math.pi / angle_count)
    radius = (jnp.arange(length, dtype=jnp.int32) - length // 2).astype(jnp.float32)
    along_x = radius[None, :] * jnp.cos(turns)[:, None]
    along_y = radius[None, :] * jnp.sin(turns)[:, None]
    return (axis_factor(along_x, length), axis_factor(along_y, length))

def exact(spec, first, second):
    return jnp.einsum(spec, first, second, precision=lax.Precision.HIGHEST)

def exact_left(mat_re, mat_im, planes):
    spec = 'jk,bkl->bjl'
    real = exact(spec, mat_re, planes[0]) - exact(spec, mat_im, planes[1])
    imag = exact(spec, mat_re, planes[1]) + exact(spec, mat_im, planes[0])
    return jnp.stack([real, imag])

def exact_right(planes, mat_re, mat_im):
    spec = '...k,kl->...l'
    real = exact(spec, planes[0], mat_re) - exact(spec, planes[1], mat_im)
    imag = exact(spec, planes[1], mat_re) + exact(spec, planes[0], mat_im)
    return jnp.stack([real, imag])

def spectrum(planes, cosine, sine):
    return exact_right(exact_left(cosine, -sine, planes), cosine, -sine)

def inverse_spectrum(planes, cosine, sine):
    return exact_right(exact_left(cosine, sine, planes), cosine, sine)

def sample_lines(grid, factor_x, factor_y):
    flat = grid.reshape(-1, grid.shape[2], grid.shape[3])

    def one_plane(plane):
        rows = exact('amx,xy->amy', factor_x, plane)
        return lax.optimization_barrier(jnp.sum(rows * factor_y, axis=2))
    result = lax.map(one_plane, flat)
    return result.reshape(grid.shape[0], grid.shape[1], factor_x.shape[0], factor_x.shape[1])

def spread_lines(lines, factor_x, factor_y, length):
    flat = lines.reshape(-1, lines.shape[2], lines.shape[3])

    def one_plane(plane):
        return exact('amx,amy->xy', factor_x, plane[:, :, None] * factor_y)
    result = lax.map(one_plane, flat)
    return result.reshape(lines.shape[0], lines.shape[1], length, length)

def line_to_view(lines, cosine, sine, sign):
    return exact_right(lines, cosine, sine) * sign

def view_to_line(views_in, cosine, sine, sign):
    return exact_right(views_in * sign, cosine, -sine)

def fast_left(mat_re, mat_im, planes):
    spec = 'jk,nkl->njl'
    real = jnp.einsum(spec, mat_re, planes[0], preferred_element_type=jnp.float32) - jnp.einsum(spec, mat_im, planes[1], preferred_element_type=jnp.float32)
    imag = jnp.einsum(spec, mat_re, planes[1], preferred_element_type=jnp.float32) + jnp.einsum(spec, mat_im, planes[0], preferred_element_type=jnp.float32)
    return jnp.stack([real, imag])

def fast_right(planes, mat_re, mat_im):
    spec = 'njk,kl->njl'
    real = jnp.einsum(spec, planes[0], mat_re, preferred_element_type=jnp.float32) - jnp.einsum(spec, planes[1], mat_im, preferred_element_type=jnp.float32)
    imag = jnp.einsum(spec, planes[1], mat_re, preferred_element_type=jnp.float32) + jnp.einsum(spec, planes[0], mat_im, preferred_element_type=jnp.float32)
    return jnp.stack([real, imag])

def patch_terms(patches, probe, measured, live, cos_half, sin_half, neg_half):
    exit_re = probe[0] * patches[0] - probe[1] * patches[1]
    exit_im = probe[0] * patches[1] + probe[1] * patches[0]
    exit_wave = jnp.stack([exit_re, exit_im]).astype(jnp.bfloat16)
    half_wave = fast_left(cos_half, neg_half, exit_wave).astype(jnp.bfloat16)
    field = fast_right(half_wave, cos_half, neg_half)
    misfit = (field[0] * field[0] + field[1] * field[1] - measured.astype(jnp.float32)) * live[:, None, None]
    pull = (field * misfit[None]).astype(jnp.bfloat16)
    back_half = fast_left(cos_half, sin_half, pull).astype(jnp.bfloat16)
    back = fast_right(back_half, cos_half, sin_half)
    grad_re = probe[0] * back[0] + probe[1] * back[1]
    grad_im = probe[0] * back[1] - probe[1] * back[0]
    probe_re = lax.optimization_barrier(jnp.sum(patches[0] * back[0] + patches[1] * back[1], axis=0))
    probe_im = lax.optimization_barrier(jnp.sum(patches[0] * back[1] - patches[1] * back[0], axis=0))
    cells = patches.shape[2] * patches.shape[3]
    power = jnp.sum(live * lax.optimization_barrier(jnp.sum(patches[0] * patches[0] + patches[1] * patches[1], axis=(1, 2)))) / cells
    return (jnp.stack([grad_re, grad_im]), jnp.stack([probe_re, probe_im]), power)

def cut_patches(planes, starts, length):
    return jax.vmap(lambda start: lax.dynamic_slice_in_dim(planes, start, length, 1), out_axes=1)(starts)

def add_patches(total, grads, starts):

    def place(slot, accum):
        start = starts[slot]
        piece = lax.dynamic_slice_in_dim(accum, start, grads.shape[2], 1)
        return lax.dynamic_update_slice_in_dim(accum, piece + grads[:, slot], start, 1)
    return lax.fori_loop(0, grads.shape[1], place, total)

def reference(object_slices, views, scaled_dual, probe, intensities, tile_rows, live_counts):
    cosine, sine = dft_tables(WIDTH)
    sign = parity_sign(WIDTH)
    factor_x, factor_y = line_factors(ANGLES, WIDTH)
    cos_half, sin_half = dft_tables(PROBE)
    neg_half = (-sin_half).astype(jnp.bfloat16)
    cos_half = cos_half.astype(jnp.bfloat16)
    sin_half = sin_half.astype(jnp.bfloat16)
    blocks = SLICES // SLICE_DEV

    def project_block(block):
        return line_to_view(sample_lines(spectrum(block, cosine, sine), factor_x, factor_y), cosine, sine, sign)

    def project_all(obj):
        split = jnp.moveaxis(obj.reshape(2, blocks, SLICE_DEV, WIDTH, WIDTH), 1, 0)
        result = lax.map(project_block, split)
        return jnp.moveaxis(result, 0, 1).reshape(2, SLICES, ANGLES, WIDTH)
    views_now = project_all(object_slices)

    def angle_terms(inputs):
        planes, measured, tiles, counts = inputs
        extended = jnp.pad(planes, ((0, 0), (0, PROBE - STEP), (0, 0)))
        slots = jnp.arange(N_SLAB * CAP, dtype=jnp.int32)
        slab_of = slots // CAP
        starts = slab_of * SLAB_ROWS + tiles * STEP
        live = (slots % CAP < counts[slab_of]).astype(jnp.float32)
        patches = cut_patches(extended, starts, PROBE)
        grads, probe_grad, power = patch_terms(patches, probe, measured, live, cos_half, sin_half, neg_half)
        total = add_patches(jnp.zeros(extended.shape, jnp.float32), grads, starts)
        return (total[:, :SLICES], probe_grad, power)
    per_angle = jnp.moveaxis(views, 2, 0)
    grads, probe_grads, powers = lax.map(angle_terms, (per_angle, intensities, tile_rows, live_counts))
    view_grad = jnp.moveaxis(grads, 0, 2)
    views_new = views - view_rate * (view_grad + penalty * (views - views_now + scaled_dual))
    probe_new = probe - probe_rate * lax.optimization_barrier(jnp.sum(probe_grads, axis=0)) / (jnp.sum(powers) + epsilon)
    residual = views_now - views_new - scaled_dual

    def back_block(block):
        lines = view_to_line(block, cosine, sine, sign)
        grid = spread_lines(lines, factor_x, factor_y, WIDTH)
        return inverse_spectrum(grid, cosine, sine)
    split = jnp.moveaxis(residual.reshape(2, blocks, SLICE_DEV, ANGLES, WIDTH), 1, 0)
    correction = jnp.moveaxis(lax.map(back_block, split), 0, 1).reshape(2, SLICES, WIDTH, WIDTH)
    object_new = object_slices - correction / ANGLES
    views_after = project_all(object_new)
    dual_new = scaled_dual + views_new - views_after
    return (object_new, views_new, dual_new, probe_new)
```

```python
import math

import jax
import jax.numpy as jnp
import ml_dtypes
import numpy as np
from jax import lax
from jax.experimental import pallas as pl
from jax.experimental.pallas import tpu as pltpu
from jax.sharding import PartitionSpec as P

SIDE = 128
HALF = SIDE // 2
STEP = 16
ANGLES = 32
SLICE_DEV = 8
ROWS = ANGLES * SLICE_DEV
CAP = 12
BATCH = 4
HALO = SIDE - STEP
N_SLAB = 4
QUARTER = ANGLES // 2

view_rate = 0.1
probe_rate = 16.0
epsilon = 1e-06

F32 = jnp.float32
BF16 = jnp.bfloat16
MESH = pl.DeviceIdType.MESH

GROUPS = [(0, 1), (2, 3), (4, 5), (6, 7), (8, 9), (10, 11), (12, 13), (14, 15), (16,)]
REACH = [16, 32, 32, 48, 64, 64, 64, 64, 64]


def dft_tables():
    counter = np.arange(SIDE)
    product = (counter[:, None] * counter[None, :] % SIDE).astype(np.float32)
    angle = product * np.float32(2.0 * math.pi / SIDE)
    factor = np.float32(1.0 / math.sqrt(SIDE))
    return (np.cos(angle) * factor).astype(np.float32), (np.sin(angle) * factor).astype(np.float32)


def split_table(table):
    high = table.astype(ml_dtypes.bfloat16)
    low = (table - high.astype(np.float32)).astype(ml_dtypes.bfloat16)
    return np.stack([high, low])


def hat(position):
    cells = np.arange(SIDE)[:, None] - HALF
    distance = np.abs(cells - position[None, :])
    return np.maximum(0.0, 1.0 - np.minimum(distance, SIDE - distance))


def tables():
    cosine, sine = dft_tables()
    shift_c, shift_s = np.roll(cosine, HALF, axis=0), np.roll(sine, HALF, axis=0)
    right = np.block([[shift_c.T, -shift_s.T], [shift_s.T, shift_c.T]])
    left = np.ascontiguousarray(right.T)
    sign = (1 - 2 * (np.arange(SIDE) % 2)).astype(np.float32)[None, :]
    to_view = np.block([[cosine * sign, sine * sign], [-sine * sign, cosine * sign]])
    half_left = np.block([[cosine, sine], [-sine, cosine]]).astype(ml_dtypes.bfloat16)
    half_right = np.block([[cosine, -sine], [sine, cosine]]).astype(ml_dtypes.bfloat16)
    radius = np.arange(SIDE) - HALF
    along = np.zeros((len(GROUPS), 2, SIDE, 2 * SIDE), np.float32)
    across = np.zeros((len(GROUPS), SIDE, 2 * SIDE), np.float32)
    for g, members in enumerate(GROUPS):
        for i, b in enumerate(members):
            lanes = slice(i * SIDE, (i + 1) * SIDE)
            row = radius * math.sin(math.pi * b / ANGLES)
            along[g, 0, :, lanes] = hat(row)
            if 0 < b < QUARTER:
                along[g, 1, :, lanes] = hat(-row)
            across[g, :, lanes] = hat(radius * math.cos(math.pi * b / ANGLES))
    return dict(
        right=split_table(right),
        left=split_table(left),
        to_view=split_table(to_view),
        to_line=np.ascontiguousarray(to_view.T).astype(ml_dtypes.bfloat16),
        half=np.stack([half_left, half_right]),
        along=along,
        along16=along.astype(ml_dtypes.bfloat16),
        across=np.concatenate([across, across], axis=1).astype(ml_dtypes.bfloat16),
        spread=np.ascontiguousarray(np.swapaxes(across, 1, 2)).astype(ml_dtypes.bfloat16),
    )


TABLE_NAMES = ["right", "left", "to_view", "to_line", "half", "along", "along16", "across", "spread"]


def dot(a, b):
    return jnp.dot(a, b, preferred_element_type=F32)


def split(x):
    high = x.astype(BF16)
    return high, (x - high.astype(F32)).astype(BF16)


def beside(x):
    return jnp.concatenate([x[: x.shape[0] // 2], x[x.shape[0] // 2 :]], axis=1)


def stacked(x):
    return jnp.concatenate([x[:, : x.shape[1] // 2], x[:, x.shape[1] // 2 :]], axis=0)


def spectrum(obj, t, out):
    def pair(i, carry):
        rows = [jnp.concatenate([obj[0, 2 * i + z], obj[1, 2 * i + z]], axis=1) for z in range(2)]
        high, low = split(jnp.concatenate(rows, axis=0))
        half = dot(high, t["right"][0]) + dot(low, t["right"][0]) + dot(high, t["right"][1])
        cols = jnp.concatenate([stacked(half[:SIDE]), stacked(half[SIDE:])], axis=1)
        high, low = split(cols)
        full = dot(t["left"][0], high) + dot(t["left"][0], low) + dot(t["left"][1], high)
        high, low = split(full)
        for z in range(2):
            for c in range(2):
                rows, lanes = slice(c * SIDE, (c + 1) * SIDE), slice(z * SIDE, (z + 1) * SIDE)
                out[c, 2 * i + z, :, :SIDE] = high[rows, lanes]
                out[c, 2 * i + z, :, SIDE:] = low[rows, lanes]
        return carry

    lax.fori_loop(0, SLICE_DEV // 2, pair, 0)


def sample(plane, c, t, put):
    depth = plane.shape[-1]
    for g, members in enumerate(GROUPS):
        lanes = len(members) * SIDE
        low, top = HALF - REACH[g], HALF + REACH[g]
        sums = [[], []]
        for z in range(SLICE_DEV):
            rows = dot(plane[c, z, low:top, :], t["across"][g, :depth, :lanes])
            for side in range(len(members)):
                weighed = rows * t["along"][g, side, low:top, :lanes]
                sums[side].append(jnp.sum(weighed, axis=0, keepdims=True))
        for side in range(len(members)):
            whole = jnp.concatenate(sums[side], axis=0)
            for i, b in enumerate(members):
                if side == 0 or b > 0:
                    put(c, QUARTER - b if side == 0 else QUARTER + b, whole[:, i * SIDE : (i + 1) * SIDE])


def spread(lines, c, t, out):
    for z in range(SLICE_DEV):
        total = None
        for g, members in enumerate(GROUPS):
            lanes = len(members) * SIDE
            low, top = HALF - REACH[g], HALF + REACH[g]
            terms = None
            for side in range(len(members)):
                picks = [lines[c, (QUARTER - b) if side == 0 else (QUARTER + b), z : z + 1, :] for b in members]
                line = jnp.concatenate(picks, axis=1).astype(BF16)
                term = t["along16"][g, side, low:top, :lanes] * line
                terms = term if terms is None else terms + term
            part = dot(terms, t["spread"][g, :lanes, :])
            if total is None:
                total = part
            else:
                edge = (part.shape[0] - total.shape[0]) // 2
                if edge:
                    total = jnp.concatenate(
                        [part[:edge], part[edge : edge + total.shape[0]] + total, part[edge + total.shape[0] :]], axis=0
                    )
                else:
                    total = part + total
        out[c, z] = total.astype(BF16)


def lines_to_views(lines, t, put):
    joined = jnp.concatenate([lines[0].reshape(ROWS, SIDE), lines[1].reshape(ROWS, SIDE)], axis=1)
    high, low = split(joined)
    result = dot(high, t["to_view"][0]) + dot(low, t["to_view"][0]) + dot(high, t["to_view"][1])
    for c in range(2):
        put(c, result[:, c * SIDE : (c + 1) * SIDE].reshape(ANGLES, SLICE_DEV, SIDE))


def correction(grid, t, put):
    def pair(i, carry):
        rows = [jnp.concatenate([grid[0, 2 * i + z], grid[1, 2 * i + z]], axis=1) for z in range(2)]
        half = dot(jnp.concatenate(rows, axis=0), t["left"][0]).astype(BF16)
        cols = jnp.concatenate([stacked(half[:SIDE]), stacked(half[SIDE:])], axis=1)
        full = dot(t["right"][0], cols) * (1.0 / ANGLES)
        for z in range(2):
            for c in range(2):
                put(c, 2 * i + z, full[c * SIDE : (c + 1) * SIDE, z * SIDE : (z + 1) * SIDE])
        return carry

    lax.fori_loop(0, SLICE_DEV // 2, pair, 0)


def patches(extended, probe, measured, starts, count, t, grads, probe_grad, power):
    probe_re, probe_im = probe[0], probe[1]
    edge = jnp.zeros((2, STEP, SIDE), F32)
    for first in range(0, CAP, BATCH):
        slots = range(first, first + BATCH)
        exits = []
        for n in slots:
            re = extended[0, pl.ds(starts[n], SIDE), :]
            im = extended[1, pl.ds(starts[n], SIDE), :]
            exits.append(jnp.concatenate([probe_re * re - probe_im * im, probe_re * im + probe_im * re], axis=0).astype(BF16))
        half = dot(t["half"][0], jnp.concatenate(exits, axis=1)).astype(BF16)
        field = dot(
            jnp.concatenate([beside(half[:, i * SIDE : (i + 1) * SIDE]) for i in range(BATCH)], axis=0), t["half"][1]
        )
        pulls = []
        for i, n in enumerate(slots):
            field_re = field[i * SIDE : (i + 1) * SIDE, :SIDE]
            field_im = field[i * SIDE : (i + 1) * SIDE, SIDE:]
            live = jnp.where(n < count, 1.0, 0.0).astype(F32)
            misfit = (field_re * field_re + field_im * field_im - measured[n].astype(F32)) * live
            pulls.append(jnp.concatenate([field_re * misfit, field_im * misfit], axis=0).astype(BF16))
        half = dot(t["half"][1], jnp.concatenate(pulls, axis=1)).astype(BF16)
        back = dot(
            jnp.concatenate([beside(half[:, i * SIDE : (i + 1) * SIDE]) for i in range(BATCH)], axis=0), t["half"][0]
        )
        sum_re = sum_im = squares = None
        for i, n in enumerate(slots):
            re = extended[0, pl.ds(starts[n], SIDE), :]
            im = extended[1, pl.ds(starts[n], SIDE), :]
            live = jnp.where(n < count, 1.0, 0.0).astype(F32)
            back_re = back[i * SIDE : (i + 1) * SIDE, :SIDE]
            back_im = back[i * SIDE : (i + 1) * SIDE, SIDE:]
            grads[n, 0, STEP : STEP + SIDE, :] = probe_re * back_re + probe_im * back_im
            grads[n, 1, STEP : STEP + SIDE, :] = probe_re * back_im - probe_im * back_re
            grads[n, :, :STEP, :] = edge
            grads[n, :, STEP + SIDE :, :] = edge
            term_re = re * back_re + im * back_im
            term_im = re * back_im - im * back_re
            square = jnp.sum((re * re + im * im).reshape(SIDE // 8, 8, SIDE), axis=0) * live
            sum_re = term_re if sum_re is None else sum_re + term_re
            sum_im = term_im if sum_im is None else sum_im + term_im
            squares = square if squares is None else squares + square
        if first:
            probe_grad[0] += sum_re
            probe_grad[1] += sum_im
            power[...] += squares
        else:
            probe_grad[0] = sum_re
            probe_grad[1] = sum_im
            power[...] = squares


def kernel(obj, views, dual, probe, measured, tiles, count, *rest):
    t = dict(zip(TABLE_NAMES, rest))
    rest = rest[len(TABLE_NAMES) :]
    obj_out, views_out, dual_out, probe_out = rest[:4]
    (
        extended, halo, grads, probe_grad, power, grad_out, grad_in, target, spec, lines, back, grid,
        came, now_send, now_came, after_send, after_came, chunk_send, chunk_came, slab_send, slab_came,
        halo_sem, grad_sem, target_sem, now_sem, after_sem, chunk_sem, slab_sem, gather_sem,
    ) = rest[4:]
    slab, ang = lax.axis_index("slab"), lax.axis_index("ang")

    def ang_peer(k):
        return lax.rem(ang + k, ANGLES)

    def slab_peer(k):
        return lax.rem(slab + k, N_SLAB)

    def each_ang(body):
        def step(k, carry):
            body(ang_peer(k))
            return carry

        lax.fori_loop(1, ANGLES, step, 0)

    def remote(src, dst, sems, to):
        return pltpu.make_async_remote_copy(
            src_ref=src, dst_ref=dst, send_sem=sems.at[0], recv_sem=sems.at[1], device_id=to, device_id_type=MESH
        )

    def block(ref, p):
        return ref.at[:, pl.ds(pl.multiple_of(p * SLICE_DEV, SLICE_DEV), SLICE_DEV), :]

    def await_bytes(ref, sem):
        pltpu.make_async_copy(ref, ref, sem).wait()

    barrier = pltpu.get_barrier_semaphore()
    each_ang(lambda p: pl.semaphore_signal(barrier, inc=1, device_id=(slab, p), device_id_type=MESH))
    for k in range(1, N_SLAB):
        pl.semaphore_signal(barrier, inc=1, device_id=(slab_peer(k), ang), device_id_type=MESH)
    pl.semaphore_wait(barrier, ANGLES - 1 + N_SLAB - 1)

    halo_copy = remote(views.at[:, :HALO, :], halo, halo_sem, (slab_peer(N_SLAB - 1), ang))
    halo_copy.start()
    spectrum(obj, t, spec)
    extended[:, : ROWS, :] = views[...]
    halo_copy.wait()
    inner = jnp.where(slab < N_SLAB - 1, 1.0, 0.0).astype(F32)
    extended[:, ROWS:, :] = halo[...] * inner

    picked = [tiles[0, n] for n in range(CAP)]
    starts = [tile * STEP for tile in picked]
    patches(extended, probe, measured, starts, count[0, 0], t, grads, probe_grad, power)

    def gathered(r):
        sums = [None, None]
        for n in range(CAP):
            at = (lax.max(lax.min(r - picked[n], SIDE // STEP), -1) + 1) * STEP
            for c in range(2):
                piece = grads[n, c, pl.ds(at, STEP), :]
                sums[c] = piece if sums[c] is None else sums[c] + piece
        return sums

    def outer(r, carry):
        sums = gathered(r + ROWS // STEP)
        for c in range(2):
            grad_out[c, pl.ds(pl.multiple_of(r * STEP, STEP), STEP), :] = sums[c]
        return carry

    lax.fori_loop(0, HALO // STEP, outer, 0)
    grad_copy = remote(grad_out, grad_in, grad_sem, (slab_peer(1), ang))
    grad_copy.start()

    def inside(r, carry):
        sums = gathered(r)
        at = pl.ds(pl.multiple_of(r * STEP, STEP), STEP)
        for c in range(2):
            target[c, at, :] = (1.0 - view_rate) * (views[c, at, :] + dual[c, at, :]) - view_rate * sums[c]
        return carry

    lax.fori_loop(0, ROWS // STEP, inside, 0)

    def send_target(p):
        remote(block(target, p), came.at[ang], target_sem, (slab, p)).start()

    ready = HALO // SLICE_DEV
    each_ang(lambda p: pl.when(p >= ready)(lambda: send_target(p)))

    for c in range(2):
        for i in range(SIDE // 8):
            chunk_send[c * (SIDE // 8) + i, :8, :] = probe_grad[c, 8 * i : 8 * i + 8, :]
            chunk_send[c * (SIDE // 8) + i, 8:, :] = power[...]
    grad_copy.wait()
    from_above = jnp.where(slab > 0, view_rate, 0.0).astype(F32)
    target[:, :HALO, :] = target[:, :HALO, :] - from_above * grad_in[...]
    each_ang(lambda p: pl.when(p < ready)(lambda: send_target(p)))
    came[ang] = target[:, pl.ds(pl.multiple_of(ang * SLICE_DEV, SLICE_DEV), SLICE_DEV), :]
    each_ang(lambda p: remote(chunk_send.at[p], chunk_came.at[ang], chunk_sem, (slab, p)).start())
    chunk_came[ang] = chunk_send[ang]

    def put_line(c, a, samples):
        lines[c, a] = samples

    def sample_now(c, carry):
        sample(spec, c, t, put_line)
        return carry

    lax.fori_loop(0, 2, sample_now, 0)

    def put_now(c, value):
        now_send[:, c] = value

    lines_to_views(lines, t, put_now)
    each_ang(lambda p: remote(now_send.at[p], block(now_came, ang), now_sem, (slab, p)).start())
    now_came[:, pl.ds(pl.multiple_of(ang * SLICE_DEV, SLICE_DEV), SLICE_DEV), :] = now_send[ang]

    await_bytes(chunk_came.at[: ANGLES - 1], chunk_sem.at[1])
    total = jnp.sum(chunk_came[...], axis=0)
    slab_send[...] = total
    for k in range(1, N_SLAB):
        remote(slab_send, slab_came.at[slab], slab_sem, (slab_peer(k), ang)).start()
    slab_came[slab] = total

    await_bytes(came.at[: ANGLES - 1], target_sem.at[1])
    joined = jnp.concatenate([came[:, c].reshape(ROWS, SIDE) for c in range(2)], axis=1).astype(BF16)
    pulled = dot(joined, t["to_line"][...])
    for c in range(2):
        back[c] = (1.0 - view_rate) * lines[c] - pulled[:, c * SIDE : (c + 1) * SIDE].reshape(ANGLES, SLICE_DEV, SIDE)

    def put_after(c, a, samples):
        lines[c, a] = lines[c, a] - samples * (1.0 / ANGLES)

    def sample_after(c, carry):
        spread(back, c, t, grid)
        sample(grid, c, t, put_after)
        return carry

    lax.fori_loop(0, 2, sample_after, 0)

    def put_views(c, value):
        after_send[:, c] = value

    lines_to_views(lines, t, put_views)
    each_ang(lambda p: remote(after_send.at[p], block(after_came, ang), after_sem, (slab, p)).start())
    after_came[:, pl.ds(pl.multiple_of(ang * SLICE_DEV, SLICE_DEV), SLICE_DEV), :] = after_send[ang]

    await_bytes(slab_came.at[: N_SLAB - 1], slab_sem.at[1])
    total = jnp.sum(slab_came[...], axis=0)
    scale = probe_rate / (jnp.sum(total[8:]) * (1.0 / (SIDE * SIDE)) + epsilon)
    mine = pl.ds(pl.multiple_of(ang * 8, 8), 8)
    probe_out[mine, :] = probe.reshape(2 * SIDE, SIDE)[mine, :] - total[:8] * scale
    each_ang(lambda p: remote(probe_out.at[mine, :], probe_out.at[mine, :], gather_sem, (slab, p)).start())

    def put_object(c, z, value):
        obj_out[c, z] = obj[c, z] - value

    correction(grid, t, put_object)

    await_bytes(block_span(now_came), now_sem.at[1])
    views_out[...] = target[...] - dual[...] + view_rate * now_came[...]
    await_bytes(block_span(after_came), after_sem.at[1])
    dual_out[...] = target[...] + view_rate * now_came[...] - after_came[...]
    await_bytes(probe_out.at[: 8 * (ANGLES - 1), :], gather_sem.at[1])

    await_bytes(came.at[: ANGLES - 1], target_sem.at[0])
    await_bytes(now_send.at[: ANGLES - 1], now_sem.at[0])
    await_bytes(after_send.at[: ANGLES - 1], after_sem.at[0])
    await_bytes(chunk_send.at[: ANGLES - 1], chunk_sem.at[0])
    await_bytes(slab_came.at[: N_SLAB - 1], slab_sem.at[0])
    await_bytes(probe_out.at[: 8 * (ANGLES - 1), :], gather_sem.at[0])


def block_span(ref):
    return ref.at[:, : SLICE_DEV * (ANGLES - 1), :]


def body(object_slices, views, scaled_dual, probe, intensities, tile_rows, live_counts):
    table = tables()
    args = [
        object_slices,
        views.reshape(2, ROWS, SIDE),
        scaled_dual.reshape(2, ROWS, SIDE),
        probe,
        intensities.reshape(CAP, SIDE, SIDE),
        tile_rows,
        live_counts,
    ] + [jnp.asarray(table[name]) for name in TABLE_NAMES]
    vmem, smem = pl.BlockSpec(memory_space=pltpu.VMEM), pl.BlockSpec(memory_space=pltpu.SMEM)
    blocks = (ANGLES, 2, SLICE_DEV, SIDE)
    dma = pltpu.SemaphoreType.DMA((2,))
    obj_new, views_new, dual_new, probe_new = pl.pallas_call(
        kernel,
        out_shape=[
            jax.ShapeDtypeStruct(object_slices.shape, F32),
            jax.ShapeDtypeStruct((2, ROWS, SIDE), F32),
            jax.ShapeDtypeStruct((2, ROWS, SIDE), F32),
            jax.ShapeDtypeStruct((2 * SIDE, SIDE), F32),
        ],
        in_specs=[vmem] * 5 + [smem] * 2 + [vmem] * len(TABLE_NAMES),
        out_specs=[vmem] * 4,
        scratch_shapes=[
            pltpu.VMEM((2, ROWS + HALO, SIDE), F32),
            pltpu.VMEM((2, HALO, SIDE), F32),
            pltpu.VMEM((CAP, 2, SIDE + 2 * STEP, SIDE), F32),
            pltpu.VMEM((2, SIDE, SIDE), F32),
            pltpu.VMEM((8, SIDE), F32),
            pltpu.VMEM((2, HALO, SIDE), F32),
            pltpu.VMEM((2, HALO, SIDE), F32),
            pltpu.VMEM((2, ROWS, SIDE), F32),
            pltpu.VMEM((2, SLICE_DEV, SIDE, 2 * SIDE), BF16),
            pltpu.VMEM((2, ANGLES, SLICE_DEV, SIDE), F32),
            pltpu.VMEM((2, ANGLES, SLICE_DEV, SIDE), F32),
            pltpu.VMEM((2, SLICE_DEV, SIDE, SIDE), BF16),
            pltpu.VMEM(blocks, F32),
            pltpu.VMEM(blocks, F32),
            pltpu.VMEM((2, ROWS, SIDE), F32),
            pltpu.VMEM(blocks, F32),
            pltpu.VMEM((2, ROWS, SIDE), F32),
            pltpu.VMEM((ANGLES, 16, SIDE), F32),
            pltpu.VMEM((ANGLES, 16, SIDE), F32),
            pltpu.VMEM((16, SIDE), F32),
            pltpu.VMEM((N_SLAB, 16, SIDE), F32),
        ]
        + [dma] * 8,
        compiler_params=pltpu.CompilerParams(collective_id=0, has_side_effects=True, vmem_limit_bytes=48 * 1024 * 1024),
    )(*args)
    return (
        obj_new,
        views_new.reshape(views.shape),
        dual_new.reshape(scaled_dual.shape),
        probe_new.reshape(probe.shape),
    )


def solution(mesh):
    in_specs = (
        P(None, ("slab", "ang"), None, None),
        P(None, "slab", "ang", None),
        P(None, "slab", "ang", None),
        P(),
        P("ang", "slab", None, None),
        P("ang", "slab"),
        P("ang", "slab"),
    )
    out_specs = (
        P(None, ("slab", "ang"), None, None),
        P(None, "slab", "ang", None),
        P(None, "slab", "ang", None),
        P(),
    )
    return jax.shard_map(body, mesh=mesh, in_specs=in_specs, out_specs=out_specs, check_vma=False)
```

```python
import math

import jax
import jax.numpy as jnp
import ml_dtypes
import numpy as np
from jax import lax
from jax.experimental import pallas as pl
from jax.experimental.pallas import tpu as pltpu
from jax.sharding import PartitionSpec as P

SIDE = 128
HALF = SIDE // 2
STEP = 16
ANGLES = 32
SLICE_DEV = 8
ROWS = ANGLES * SLICE_DEV
CAP = 12
BATCH = 4
HALO = SIDE - STEP
N_SLAB = 4
QUARTER = ANGLES // 2

view_rate = 0.1
probe_rate = 16.0
epsilon = 1e-06

F32 = jnp.float32
BF16 = jnp.bfloat16
MESH = pl.DeviceIdType.MESH

GROUPS = [(0, 1), (2, 3), (4, 5), (6, 7), (8, 9), (10, 11), (12, 13), (14, 15), (16,)]
REACH = [16, 32, 32, 48, 64, 64, 64, 64, 64]


def dft_tables():
    counter = np.arange(SIDE)
    product = (counter[:, None] * counter[None, :] % SIDE).astype(np.float32)
    angle = product * np.float32(2.0 * math.pi / SIDE)
    factor = np.float32(1.0 / math.sqrt(SIDE))
    return (np.cos(angle) * factor).astype(np.float32), (np.sin(angle) * factor).astype(np.float32)


def split_table(table):
    high = table.astype(ml_dtypes.bfloat16)
    low = (table - high.astype(np.float32)).astype(ml_dtypes.bfloat16)
    return np.stack([high, low])


def hat(position):
    cells = np.arange(SIDE)[:, None] - HALF
    distance = np.abs(cells - position[None, :])
    return np.maximum(0.0, 1.0 - np.minimum(distance, SIDE - distance))


def tables():
    cosine, sine = dft_tables()
    shift_c, shift_s = np.roll(cosine, HALF, axis=0), np.roll(sine, HALF, axis=0)
    right = np.block([[shift_c.T, -shift_s.T], [shift_s.T, shift_c.T]])
    left = np.ascontiguousarray(right.T)
    sign = (1 - 2 * (np.arange(SIDE) % 2)).astype(np.float32)[None, :]
    to_view = np.block([[cosine * sign, sine * sign], [-sine * sign, cosine * sign]])
    half_left = np.block([[cosine, sine], [-sine, cosine]]).astype(ml_dtypes.bfloat16)
    half_right = np.block([[cosine, -sine], [sine, cosine]]).astype(ml_dtypes.bfloat16)
    radius = np.arange(SIDE) - HALF
    along = np.zeros((len(GROUPS), 2, SIDE, 2 * SIDE), np.float32)
    across = np.zeros((len(GROUPS), SIDE, 2 * SIDE), np.float32)
    for g, members in enumerate(GROUPS):
        for i, b in enumerate(members):
            lanes = slice(i * SIDE, (i + 1) * SIDE)
            row = radius * math.sin(math.pi * b / ANGLES)
            along[g, 0, :, lanes] = hat(row)
            if 0 < b < QUARTER:
                along[g, 1, :, lanes] = hat(-row)
            across[g, :, lanes] = hat(radius * math.cos(math.pi * b / ANGLES))
    return dict(
        right=split_table(right),
        left=split_table(left),
        to_view=split_table(to_view),
        to_line=np.ascontiguousarray(to_view.T).astype(ml_dtypes.bfloat16),
        half=np.stack([half_left, half_right]),
        along=along,
        along16=along.astype(ml_dtypes.bfloat16),
        across=np.concatenate([across, across], axis=1).astype(ml_dtypes.bfloat16),
        spread=np.ascontiguousarray(np.swapaxes(across, 1, 2)).astype(ml_dtypes.bfloat16),
    )


TABLE_NAMES = ["right", "left", "to_view", "to_line", "half", "along", "along16", "across", "spread"]


def dot(a, b):
    return jnp.dot(a, b, preferred_element_type=F32)


def split(x):
    high = x.astype(BF16)
    return high, (x - high.astype(F32)).astype(BF16)


def beside(x):
    return jnp.concatenate([x[: x.shape[0] // 2], x[x.shape[0] // 2 :]], axis=1)


def stacked(x):
    return jnp.concatenate([x[:, : x.shape[1] // 2], x[:, x.shape[1] // 2 :]], axis=0)


def spectrum(obj, t, out):
    for i in range(SLICE_DEV // 2):
        rows = [jnp.concatenate([obj[0, 2 * i + z], obj[1, 2 * i + z]], axis=1) for z in range(2)]
        high, low = split(jnp.concatenate(rows, axis=0))
        half = dot(high, t["right"][0]) + dot(low, t["right"][0]) + dot(high, t["right"][1])
        cols = jnp.concatenate([stacked(half[:SIDE]), stacked(half[SIDE:])], axis=1)
        high, low = split(cols)
        full = dot(t["left"][0], high) + dot(t["left"][0], low) + dot(t["left"][1], high)
        high, low = split(full)
        for z in range(2):
            for c in range(2):
                rows, lanes = slice(c * SIDE, (c + 1) * SIDE), slice(z * SIDE, (z + 1) * SIDE)
                out[c, 2 * i + z, :, :SIDE] = high[rows, lanes]
                out[c, 2 * i + z, :, SIDE:] = low[rows, lanes]


def sample(plane, c, t, put):
    depth = plane.shape[-1]
    for g, members in enumerate(GROUPS):
        lanes = len(members) * SIDE
        low, top = HALF - REACH[g], HALF + REACH[g]
        sums = [[], []]
        for z in range(SLICE_DEV):
            rows = dot(plane[c, z, low:top, :], t["across"][g, :depth, :lanes])
            for side in range(len(members)):
                weighed = rows * t["along"][g, side, low:top, :lanes]
                sums[side].append(jnp.sum(weighed, axis=0, keepdims=True))
        for side in range(len(members)):
            whole = jnp.concatenate(sums[side], axis=0)
            for i, b in enumerate(members):
                if side == 0 or b > 0:
                    put(c, QUARTER - b if side == 0 else QUARTER + b, whole[:, i * SIDE : (i + 1) * SIDE])


def spread(lines, c, t, out):
    for z in range(SLICE_DEV):
        total = None
        for g, members in enumerate(GROUPS):
            lanes = len(members) * SIDE
            low, top = HALF - REACH[g], HALF + REACH[g]
            terms = None
            for side in range(len(members)):
                picks = [lines[c, (QUARTER - b) if side == 0 else (QUARTER + b), z : z + 1, :] for b in members]
                line = jnp.concatenate(picks, axis=1).astype(BF16)
                term = t["along16"][g, side, low:top, :lanes] * line
                terms = term if terms is None else terms + term
            part = dot(terms, t["spread"][g, :lanes, :])
            if total is None:
                total = part
            else:
                edge = (part.shape[0] - total.shape[0]) // 2
                if edge:
                    total = jnp.concatenate(
                        [part[:edge], part[edge : edge + total.shape[0]] + total, part[edge + total.shape[0] :]], axis=0
                    )
                else:
                    total = part + total
        out[c, z] = total.astype(BF16)


def lines_to_views(lines, t, put):
    joined = jnp.concatenate([lines[0].reshape(ROWS, SIDE), lines[1].reshape(ROWS, SIDE)], axis=1)
    high, low = split(joined)
    result = dot(high, t["to_view"][0]) + dot(low, t["to_view"][0]) + dot(high, t["to_view"][1])
    for c in range(2):
        put(c, result[:, c * SIDE : (c + 1) * SIDE].reshape(ANGLES, SLICE_DEV, SIDE))


def correction(grid, t, put):
    for i in range(SLICE_DEV // 2):
        rows = [jnp.concatenate([grid[0, 2 * i + z], grid[1, 2 * i + z]], axis=1) for z in range(2)]
        half = dot(jnp.concatenate(rows, axis=0), t["left"][0]).astype(BF16)
        cols = jnp.concatenate([stacked(half[:SIDE]), stacked(half[SIDE:])], axis=1)
        full = dot(t["right"][0], cols) * (1.0 / ANGLES)
        for z in range(2):
            for c in range(2):
                put(c, 2 * i + z, full[c * SIDE : (c + 1) * SIDE, z * SIDE : (z + 1) * SIDE])


def patches(extended, probe, measured, starts, count, t, grads, probe_grad, power):
    probe_re, probe_im = probe[0], probe[1]
    edge = jnp.zeros((2, STEP, SIDE), F32)
    for first in range(0, CAP, BATCH):
        slots = range(first, first + BATCH)
        exits = []
        for n in slots:
            re = extended[0, pl.ds(starts[n], SIDE), :]
            im = extended[1, pl.ds(starts[n], SIDE), :]
            exits.append(jnp.concatenate([probe_re * re - probe_im * im, probe_re * im + probe_im * re], axis=0).astype(BF16))
        half = dot(t["half"][0], jnp.concatenate(exits, axis=1)).astype(BF16)
        field = dot(
            jnp.concatenate([beside(half[:, i * SIDE : (i + 1) * SIDE]) for i in range(BATCH)], axis=0), t["half"][1]
        )
        pulls = []
        for i, n in enumerate(slots):
            field_re = field[i * SIDE : (i + 1) * SIDE, :SIDE]
            field_im = field[i * SIDE : (i + 1) * SIDE, SIDE:]
            live = jnp.where(n < count, 1.0, 0.0).astype(F32)
            misfit = (field_re * field_re + field_im * field_im - measured[n].astype(F32)) * live
            pulls.append(jnp.concatenate([field_re * misfit, field_im * misfit], axis=0).astype(BF16))
        half = dot(t["half"][1], jnp.concatenate(pulls, axis=1)).astype(BF16)
        back = dot(
            jnp.concatenate([beside(half[:, i * SIDE : (i + 1) * SIDE]) for i in range(BATCH)], axis=0), t["half"][0]
        )
        sum_re = sum_im = squares = None
        for i, n in enumerate(slots):
            re = extended[0, pl.ds(starts[n], SIDE), :]
            im = extended[1, pl.ds(starts[n], SIDE), :]
            live = jnp.where(n < count, 1.0, 0.0).astype(F32)
            back_re = back[i * SIDE : (i + 1) * SIDE, :SIDE]
            back_im = back[i * SIDE : (i + 1) * SIDE, SIDE:]
            grads[n, 0, STEP : STEP + SIDE, :] = probe_re * back_re + probe_im * back_im
            grads[n, 1, STEP : STEP + SIDE, :] = probe_re * back_im - probe_im * back_re
            grads[n, :, :STEP, :] = edge
            grads[n, :, STEP + SIDE :, :] = edge
            term_re = re * back_re + im * back_im
            term_im = re * back_im - im * back_re
            square = jnp.sum((re * re + im * im).reshape(SIDE // 8, 8, SIDE), axis=0) * live
            sum_re = term_re if sum_re is None else sum_re + term_re
            sum_im = term_im if sum_im is None else sum_im + term_im
            squares = square if squares is None else squares + square
        if first:
            probe_grad[0] += sum_re
            probe_grad[1] += sum_im
            power[...] += squares
        else:
            probe_grad[0] = sum_re
            probe_grad[1] = sum_im
            power[...] = squares


LOADED = ["views", "dual", "obj", "probe", "measured"] + TABLE_NAMES
LOAD_ORDER = ["views", "obj", "right", "left", "probe", "measured", "half", "dual"] + [
    "across", "along", "to_view", "to_line", "along16", "spread"
]


def kernel(tiles, count, *rest):
    far = dict(zip(LOADED, rest))
    rest = rest[len(LOADED) :]
    obj_out, views_out, dual_out, probe_out = rest[:4]
    rest = rest[4:]
    near = dict(zip(LOADED[1:], rest))
    (
        extended, grads, probe_grad, power, grad_out, grad_in, target, spec, lines, back, grid,
        came, now_send, now_came, after_send, after_came, chunk_send, chunk_came, slab_send, slab_came,
        halo_sem, grad_sem, target_sem, now_sem, after_sem, chunk_sem, slab_sem, gather_sem, load_sem,
    ) = rest[len(LOADED) - 1 :]
    obj, dual, probe, measured = (near[name] for name in ("obj", "dual", "probe", "measured"))
    t = near
    slab, ang = lax.axis_index("slab"), lax.axis_index("ang")

    def ang_peer(k):
        return lax.rem(ang + k, ANGLES)

    def slab_peer(k):
        return lax.rem(slab + k, N_SLAB)

    def each_ang(body):
        def step(k, carry):
            body(ang_peer(k))
            return carry

        lax.fori_loop(1, ANGLES, step, 0)

    def remote(src, dst, sems, to):
        return pltpu.make_async_remote_copy(
            src_ref=src, dst_ref=dst, send_sem=sems.at[0], recv_sem=sems.at[1], device_id=to, device_id_type=MESH
        )

    def block(ref, p):
        return ref.at[:, pl.ds(pl.multiple_of(p * SLICE_DEV, SLICE_DEV), SLICE_DEV), :]

    def await_bytes(ref, sem):
        pltpu.make_async_copy(ref, ref, sem).wait()

    near["views"] = extended.at[:, :ROWS, :]
    loads = {}
    for name in LOAD_ORDER:
        loads[name] = pltpu.make_async_copy(far[name], near[name], load_sem.at[LOAD_ORDER.index(name)])
    barrier = pltpu.get_barrier_semaphore()
    each_ang(lambda p: pl.semaphore_signal(barrier, inc=1, device_id=(slab, p), device_id_type=MESH))
    for k in range(1, N_SLAB):
        pl.semaphore_signal(barrier, inc=1, device_id=(slab_peer(k), ang), device_id_type=MESH)
    for name in LOAD_ORDER:
        loads[name].start()
    pl.semaphore_wait(barrier, ANGLES - 1 + N_SLAB - 1)

    loads["views"].wait()
    halo_copy = remote(
        extended.at[:, :HALO, :], extended.at[:, ROWS:, :], halo_sem, (slab_peer(N_SLAB - 1), ang)
    )
    halo_copy.start()
    for name in ("obj", "right", "left"):
        loads[name].wait()
    spectrum(obj, t, spec)
    for name in ("probe", "measured", "half", "dual"):
        loads[name].wait()
    halo_copy.wait()
    inner = jnp.where(slab < N_SLAB - 1, 1.0, 0.0).astype(F32)
    extended[:, ROWS:, :] = extended[:, ROWS:, :] * inner

    picked = [tiles[0, n] for n in range(CAP)]
    starts = [tile * STEP for tile in picked]
    patches(extended, probe, measured, starts, count[0, 0], t, grads, probe_grad, power)

    def gathered(r):
        sums = [None, None]
        for n in range(CAP):
            at = (lax.max(lax.min(r - picked[n], SIDE // STEP), -1) + 1) * STEP
            for c in range(2):
                piece = grads[n, c, pl.ds(at, STEP), :]
                sums[c] = piece if sums[c] is None else sums[c] + piece
        return sums

    def outer(r, carry):
        sums = gathered(r + ROWS // STEP)
        for c in range(2):
            grad_out[c, pl.ds(pl.multiple_of(r * STEP, STEP), STEP), :] = sums[c]
        return carry

    lax.fori_loop(0, HALO // STEP, outer, 0)
    grad_copy = remote(grad_out, grad_in, grad_sem, (slab_peer(1), ang))
    grad_copy.start()

    def inside(r, carry):
        sums = gathered(r)
        at = pl.ds(pl.multiple_of(r * STEP, STEP), STEP)
        for c in range(2):
            target[c, at, :] = (1.0 - view_rate) * (extended[c, at, :] + dual[c, at, :]) - view_rate * sums[c]
        return carry

    lax.fori_loop(0, ROWS // STEP, inside, 0)

    def send_target(p):
        remote(block(target, p), came.at[ang], target_sem, (slab, p)).start()

    ready = HALO // SLICE_DEV
    each_ang(lambda p: pl.when(p >= ready)(lambda: send_target(p)))

    for c in range(2):
        for i in range(SIDE // 8):
            chunk_send[c * (SIDE // 8) + i, :8, :] = probe_grad[c, 8 * i : 8 * i + 8, :]
            chunk_send[c * (SIDE // 8) + i, 8:, :] = power[...]
    grad_copy.wait()
    from_above = jnp.where(slab > 0, view_rate, 0.0).astype(F32)
    target[:, :HALO, :] = target[:, :HALO, :] - from_above * grad_in[...]
    each_ang(lambda p: pl.when(p < ready)(lambda: send_target(p)))
    came[ang] = target[:, pl.ds(pl.multiple_of(ang * SLICE_DEV, SLICE_DEV), SLICE_DEV), :]
    each_ang(lambda p: remote(chunk_send.at[p], chunk_came.at[ang], chunk_sem, (slab, p)).start())
    chunk_came[ang] = chunk_send[ang]

    for name in ("across", "along", "to_view", "to_line", "along16", "spread"):
        loads[name].wait()

    def put_line(c, a, samples):
        lines[c, a] = samples

    def sample_now(c, carry):
        sample(spec, c, t, put_line)
        return carry

    lax.fori_loop(0, 2, sample_now, 0)

    def put_now(c, value):
        now_send[:, c] = value

    lines_to_views(lines, t, put_now)
    each_ang(lambda p: remote(now_send.at[p], block(now_came, ang), now_sem, (slab, p)).start())
    now_came[:, pl.ds(pl.multiple_of(ang * SLICE_DEV, SLICE_DEV), SLICE_DEV), :] = now_send[ang]

    await_bytes(chunk_came.at[: ANGLES - 1], chunk_sem.at[1])
    total = jnp.sum(chunk_came[...], axis=0)
    slab_send[...] = total
    for k in range(1, N_SLAB):
        remote(slab_send, slab_came.at[slab], slab_sem, (slab_peer(k), ang)).start()
    slab_came[slab] = total

    await_bytes(came.at[: ANGLES - 1], target_sem.at[1])
    joined = jnp.concatenate([came[:, c].reshape(ROWS, SIDE) for c in range(2)], axis=1).astype(BF16)
    pulled = dot(joined, t["to_line"][...])
    for c in range(2):
        back[c] = (1.0 - view_rate) * lines[c] - pulled[:, c * SIDE : (c + 1) * SIDE].reshape(ANGLES, SLICE_DEV, SIDE)

    def put_after(c, a, samples):
        lines[c, a] = lines[c, a] - samples * (1.0 / ANGLES)

    def sample_after(c, carry):
        spread(back, c, t, grid)
        sample(grid, c, t, put_after)
        return carry

    lax.fori_loop(0, 2, sample_after, 0)

    def put_views(c, value):
        after_send[:, c] = value

    lines_to_views(lines, t, put_views)
    each_ang(lambda p: remote(after_send.at[p], block(after_came, ang), after_sem, (slab, p)).start())
    after_came[:, pl.ds(pl.multiple_of(ang * SLICE_DEV, SLICE_DEV), SLICE_DEV), :] = after_send[ang]

    await_bytes(slab_came.at[: N_SLAB - 1], slab_sem.at[1])
    total = jnp.sum(slab_came[...], axis=0)
    scale = probe_rate / (jnp.sum(total[8:]) * (1.0 / (SIDE * SIDE)) + epsilon)
    mine = pl.ds(pl.multiple_of(ang * 8, 8), 8)
    probe_out[mine, :] = probe.reshape(2 * SIDE, SIDE)[mine, :] - total[:8] * scale
    each_ang(lambda p: remote(probe_out.at[mine, :], probe_out.at[mine, :], gather_sem, (slab, p)).start())

    def put_object(c, z, value):
        obj_out[c, z] = obj[c, z] - value

    correction(grid, t, put_object)
    await_bytes(block_span(now_came), now_sem.at[1])
    views_out[...] = target[...] - dual[...] + view_rate * now_came[...]
    await_bytes(probe_out.at[: 8 * (ANGLES - 1), :], gather_sem.at[1])
    await_bytes(block_span(after_came), after_sem.at[1])
    dual_out[...] = target[...] + view_rate * now_came[...] - after_came[...]

    await_bytes(came.at[: ANGLES - 1], target_sem.at[0])
    await_bytes(now_send.at[: ANGLES - 1], now_sem.at[0])
    await_bytes(after_send.at[: ANGLES - 1], after_sem.at[0])
    await_bytes(chunk_send.at[: ANGLES - 1], chunk_sem.at[0])
    await_bytes(slab_came.at[: N_SLAB - 1], slab_sem.at[0])
    await_bytes(probe_out.at[: 8 * (ANGLES - 1), :], gather_sem.at[0])


def store_all(*refs):
    copies = [pltpu.make_async_copy(refs[i], refs[4 + i], refs[8].at[i]) for i in range(4)]
    for copy in copies:
        copy.start()
    for copy in copies:
        copy.wait()


def block_span(ref):
    return ref.at[:, : SLICE_DEV * (ANGLES - 1), :]


def body(object_slices, views, scaled_dual, probe, intensities, tile_rows, live_counts):
    table = tables()
    arrays = dict(
        views=views.reshape(2, ROWS, SIDE),
        dual=scaled_dual.reshape(2, ROWS, SIDE),
        obj=object_slices,
        probe=probe,
        measured=intensities.reshape(CAP, SIDE, SIDE),
        **{name: jnp.asarray(table[name]) for name in TABLE_NAMES},
    )
    far, smem = pl.BlockSpec(memory_space=pltpu.HBM), pl.BlockSpec(memory_space=pltpu.SMEM)
    blocks = (ANGLES, 2, SLICE_DEV, SIDE)
    dma = pltpu.SemaphoreType.DMA((2,))
    scratch = [pltpu.VMEM(arrays[name].shape, arrays[name].dtype) for name in LOADED[1:]] + [
        pltpu.VMEM((2, ROWS + HALO, SIDE), F32),
        pltpu.VMEM((CAP, 2, SIDE + 2 * STEP, SIDE), F32),
        pltpu.VMEM((2, SIDE, SIDE), F32),
        pltpu.VMEM((8, SIDE), F32),
        pltpu.VMEM((2, HALO, SIDE), F32),
        pltpu.VMEM((2, HALO, SIDE), F32),
        pltpu.VMEM((2, ROWS, SIDE), F32),
        pltpu.VMEM((2, SLICE_DEV, SIDE, 2 * SIDE), BF16),
        pltpu.VMEM((2, ANGLES, SLICE_DEV, SIDE), F32),
        pltpu.VMEM((2, ANGLES, SLICE_DEV, SIDE), F32),
        pltpu.VMEM((2, SLICE_DEV, SIDE, SIDE), BF16),
        pltpu.VMEM(blocks, F32),
        pltpu.VMEM(blocks, F32),
        pltpu.VMEM((2, ROWS, SIDE), F32),
        pltpu.VMEM(blocks, F32),
        pltpu.VMEM((2, ROWS, SIDE), F32),
        pltpu.VMEM((ANGLES, 16, SIDE), F32),
        pltpu.VMEM((ANGLES, 16, SIDE), F32),
        pltpu.VMEM((16, SIDE), F32),
        pltpu.VMEM((N_SLAB, 16, SIDE), F32),
    ]
    near = pl.BlockSpec(memory_space=pltpu.VMEM)
    results = [
        jax.ShapeDtypeStruct(object_slices.shape, F32),
        jax.ShapeDtypeStruct((2, ROWS, SIDE), F32),
        jax.ShapeDtypeStruct((2, ROWS, SIDE), F32),
        jax.ShapeDtypeStruct((2 * SIDE, SIDE), F32),
    ]
    made = pl.pallas_call(
        kernel,
        out_shape=results,
        in_specs=[smem] * 2 + [far] * len(LOADED),
        out_specs=[near] * 4,
        scratch_shapes=scratch
        + [dma] * 8
        + [pltpu.SemaphoreType.DMA((len(LOADED),))],
        compiler_params=pltpu.CompilerParams(collective_id=0, has_side_effects=True, vmem_limit_bytes=56 * 1024 * 1024),
    )(tile_rows, live_counts, *[arrays[name] for name in LOADED])
    obj_new, views_new, dual_new, probe_new = pl.pallas_call(
        store_all,
        out_shape=results,
        in_specs=[near] * 4,
        out_specs=[far] * 4,
        scratch_shapes=[pltpu.SemaphoreType.DMA((4,))],
    )(*made)
    return (
        obj_new,
        views_new.reshape(views.shape),
        dual_new.reshape(scaled_dual.shape),
        probe_new.reshape(probe.shape),
    )


def solution(mesh):
    in_specs = (
        P(None, ("slab", "ang"), None, None),
        P(None, "slab", "ang", None),
        P(None, "slab", "ang", None),
        P(),
        P("ang", "slab", None, None),
        P("ang", "slab"),
        P("ang", "slab"),
    )
    out_specs = (
        P(None, ("slab", "ang"), None, None),
        P(None, "slab", "ang", None),
        P(None, "slab", "ang", None),
        P(),
    )
    return jax.shard_map(body, mesh=mesh, in_specs=in_specs, out_specs=out_specs, check_vma=False)
```

```python
import math

import jax
import jax.numpy as jnp
import ml_dtypes
import numpy as np
from jax import lax
from jax.experimental import pallas as pl
from jax.experimental.pallas import tpu as pltpu
from jax.sharding import PartitionSpec as P

SIDE = 128
HALF = SIDE // 2
STEP = 16
ANGLES = 32
SLICE_DEV = 8
ROWS = ANGLES * SLICE_DEV
CAP = 12
BATCH = 4
HALO = SIDE - STEP
N_SLAB = 4
QUARTER = ANGLES // 2

view_rate = 0.1
probe_rate = 16.0
epsilon = 1e-06

F32 = jnp.float32
BF16 = jnp.bfloat16
MESH = pl.DeviceIdType.MESH

GROUPS = [(0, 1), (2, 3), (4, 5), (6, 7), (8, 9), (10, 11), (12, 13), (14, 15), (16,)]
OFFSETS = sorted(
    [(x, y, core) for x in range(4) for y in range(4) for core in range(2)][1:],
    key=lambda o: -(min(o[0], 4 - o[0]) + min(o[1], 4 - o[1])),
)
REACH = [16, 32, 32, 48, 64, 64, 64, 64, 64]


def dft_tables():
    counter = np.arange(SIDE)
    product = (counter[:, None] * counter[None, :] % SIDE).astype(np.float32)
    angle = product * np.float32(2.0 * math.pi / SIDE)
    factor = np.float32(1.0 / math.sqrt(SIDE))
    return (np.cos(angle) * factor).astype(np.float32), (np.sin(angle) * factor).astype(np.float32)


def split_table(table):
    high = table.astype(ml_dtypes.bfloat16)
    low = (table - high.astype(np.float32)).astype(ml_dtypes.bfloat16)
    return np.stack([high, low])


def hat(position):
    cells = np.arange(SIDE)[:, None] - HALF
    distance = np.abs(cells - position[None, :])
    return np.maximum(0.0, 1.0 - np.minimum(distance, SIDE - distance))


def tables():
    cosine, sine = dft_tables()
    shift_c, shift_s = np.roll(cosine, HALF, axis=0), np.roll(sine, HALF, axis=0)
    right = np.block([[shift_c.T, -shift_s.T], [shift_s.T, shift_c.T]])
    left = np.ascontiguousarray(right.T)
    sign = (1 - 2 * (np.arange(SIDE) % 2)).astype(np.float32)[None, :]
    to_view = np.block([[cosine * sign, sine * sign], [-sine * sign, cosine * sign]])
    half_left = np.block([[cosine, sine], [-sine, cosine]]).astype(ml_dtypes.bfloat16)
    half_right = np.block([[cosine, -sine], [sine, cosine]]).astype(ml_dtypes.bfloat16)
    radius = np.arange(SIDE) - HALF
    along = np.zeros((len(GROUPS), 2, SIDE, 2 * SIDE), np.float32)
    across = np.zeros((len(GROUPS), SIDE, 2 * SIDE), np.float32)
    for g, members in enumerate(GROUPS):
        for i, b in enumerate(members):
            lanes = slice(i * SIDE, (i + 1) * SIDE)
            row = radius * math.sin(math.pi * b / ANGLES)
            along[g, 0, :, lanes] = hat(row)
            if 0 < b < QUARTER:
                along[g, 1, :, lanes] = hat(-row)
            across[g, :, lanes] = hat(radius * math.cos(math.pi * b / ANGLES))
    return dict(
        right=split_table(right),
        left=split_table(left),
        to_view=split_table(to_view),
        to_line=np.ascontiguousarray(to_view.T).astype(ml_dtypes.bfloat16),
        half=np.stack([half_left, half_right]),
        along=along,
        along16=along.astype(ml_dtypes.bfloat16),
        across=np.concatenate([across, across], axis=1).astype(ml_dtypes.bfloat16),
        spread=np.ascontiguousarray(np.swapaxes(across, 1, 2)).astype(ml_dtypes.bfloat16),
    )


TABLE_NAMES = ["right", "left", "to_view", "to_line", "half", "along", "along16", "across", "spread"]


def dot(a, b):
    return jnp.dot(a, b, preferred_element_type=F32)


def split(x):
    high = x.astype(BF16)
    return high, (x - high.astype(F32)).astype(BF16)


def beside(x):
    return jnp.concatenate([x[: x.shape[0] // 2], x[x.shape[0] // 2 :]], axis=1)


def stacked(x):
    return jnp.concatenate([x[:, : x.shape[1] // 2], x[:, x.shape[1] // 2 :]], axis=0)


def spectrum(obj, t, out):
    for i in range(SLICE_DEV // 2):
        rows = [jnp.concatenate([obj[0, 2 * i + z], obj[1, 2 * i + z]], axis=1) for z in range(2)]
        high, low = split(jnp.concatenate(rows, axis=0))
        half = dot(high, t["right"][0]) + dot(low, t["right"][0]) + dot(high, t["right"][1])
        cols = jnp.concatenate([stacked(half[:SIDE]), stacked(half[SIDE:])], axis=1)
        high, low = split(cols)
        full = dot(t["left"][0], high) + dot(t["left"][0], low) + dot(t["left"][1], high)
        high, low = split(full)
        for z in range(2):
            for c in range(2):
                rows, lanes = slice(c * SIDE, (c + 1) * SIDE), slice(z * SIDE, (z + 1) * SIDE)
                out[c, 2 * i + z, :, :SIDE] = high[rows, lanes]
                out[c, 2 * i + z, :, SIDE:] = low[rows, lanes]


def sample(plane, c, t, put):
    depth = plane.shape[-1]
    for g, members in enumerate(GROUPS):
        lanes = len(members) * SIDE
        low, top = HALF - REACH[g], HALF + REACH[g]
        sums = [[], []]
        for z in range(SLICE_DEV):
            rows = dot(plane[c, z, low:top, :], t["across"][g, :depth, :lanes])
            for side in range(len(members)):
                weighed = rows * t["along"][g, side, low:top, :lanes]
                sums[side].append(jnp.sum(weighed, axis=0, keepdims=True))
        for side in range(len(members)):
            whole = jnp.concatenate(sums[side], axis=0)
            for i, b in enumerate(members):
                if side == 0 or b > 0:
                    put(c, QUARTER - b if side == 0 else QUARTER + b, whole[:, i * SIDE : (i + 1) * SIDE])


def spread(lines, c, t, out):
    for z in range(SLICE_DEV):
        total = None
        for g, members in enumerate(GROUPS):
            lanes = len(members) * SIDE
            low, top = HALF - REACH[g], HALF + REACH[g]
            terms = None
            for side in range(len(members)):
                picks = [lines[c, (QUARTER - b) if side == 0 else (QUARTER + b), z : z + 1, :] for b in members]
                line = jnp.concatenate(picks, axis=1).astype(BF16)
                term = t["along16"][g, side, low:top, :lanes] * line
                terms = term if terms is None else terms + term
            part = dot(terms, t["spread"][g, :lanes, :])
            if total is None:
                total = part
            else:
                edge = (part.shape[0] - total.shape[0]) // 2
                if edge:
                    total = jnp.concatenate(
                        [part[:edge], part[edge : edge + total.shape[0]] + total, part[edge + total.shape[0] :]], axis=0
                    )
                else:
                    total = part + total
        out[c, z] = total.astype(BF16)


def lines_to_views(lines, t, put):
    joined = jnp.concatenate([lines[0].reshape(ROWS, SIDE), lines[1].reshape(ROWS, SIDE)], axis=1)
    high, low = split(joined)
    result = dot(high, t["to_view"][0]) + dot(low, t["to_view"][0]) + dot(high, t["to_view"][1])
    for c in range(2):
        put(c, result[:, c * SIDE : (c + 1) * SIDE].reshape(ANGLES, SLICE_DEV, SIDE))


def correction(grid, t, put):
    for i in range(SLICE_DEV // 2):
        rows = [jnp.concatenate([grid[0, 2 * i + z], grid[1, 2 * i + z]], axis=1) for z in range(2)]
        half = dot(jnp.concatenate(rows, axis=0), t["left"][0]).astype(BF16)
        cols = jnp.concatenate([stacked(half[:SIDE]), stacked(half[SIDE:])], axis=1)
        full = dot(t["right"][0], cols) * (1.0 / ANGLES)
        for z in range(2):
            for c in range(2):
                put(c, 2 * i + z, full[c * SIDE : (c + 1) * SIDE, z * SIDE : (z + 1) * SIDE])


def patches(extended, probe, measured, starts, count, t, grads, chunks, power):
    probe_re, probe_im = probe[0], probe[1]
    edge = jnp.zeros((2, STEP, SIDE), F32)
    for first in range(0, CAP, BATCH):
        slots = range(first, first + BATCH)
        exits = []
        for n in slots:
            re = extended[0, pl.ds(starts[n], SIDE), :]
            im = extended[1, pl.ds(starts[n], SIDE), :]
            exits.append(jnp.concatenate([probe_re * re - probe_im * im, probe_re * im + probe_im * re], axis=0).astype(BF16))
        half = dot(t["half"][0], jnp.concatenate(exits, axis=1)).astype(BF16)
        field = dot(
            jnp.concatenate([beside(half[:, i * SIDE : (i + 1) * SIDE]) for i in range(BATCH)], axis=0), t["half"][1]
        )
        pulls = []
        for i, n in enumerate(slots):
            field_re = field[i * SIDE : (i + 1) * SIDE, :SIDE]
            field_im = field[i * SIDE : (i + 1) * SIDE, SIDE:]
            live = jnp.where(n < count, 1.0, 0.0).astype(F32)
            misfit = (field_re * field_re + field_im * field_im - measured[n].astype(F32)) * live
            pulls.append(jnp.concatenate([field_re * misfit, field_im * misfit], axis=0).astype(BF16))
        half = dot(t["half"][1], jnp.concatenate(pulls, axis=1)).astype(BF16)
        back = dot(
            jnp.concatenate([beside(half[:, i * SIDE : (i + 1) * SIDE]) for i in range(BATCH)], axis=0), t["half"][0]
        )
        sum_re = sum_im = squares = None
        for i, n in enumerate(slots):
            re = extended[0, pl.ds(starts[n], SIDE), :]
            im = extended[1, pl.ds(starts[n], SIDE), :]
            live = jnp.where(n < count, 1.0, 0.0).astype(F32)
            back_re = back[i * SIDE : (i + 1) * SIDE, :SIDE]
            back_im = back[i * SIDE : (i + 1) * SIDE, SIDE:]
            grads[n, 0, STEP : STEP + SIDE, :] = probe_re * back_re + probe_im * back_im
            grads[n, 1, STEP : STEP + SIDE, :] = probe_re * back_im - probe_im * back_re
            grads[n, :, :STEP, :] = edge
            grads[n, :, STEP + SIDE :, :] = edge
            term_re = re * back_re + im * back_im
            term_im = re * back_im - im * back_re
            square = jnp.sum((re * re + im * im).reshape(SIDE // 8, 8, SIDE), axis=0) * live
            sum_re = term_re if sum_re is None else sum_re + term_re
            sum_im = term_im if sum_im is None else sum_im + term_im
            squares = square if squares is None else squares + square
        for i in range(ANGLES):
            part = (sum_re, sum_im)[i // 16][(i % 16) * 8 : (i % 16 + 1) * 8]
            chunks[i] = chunks[i] + part if first else part
        power[...] = power[...] + squares if first else squares


LOADED = ["views", "dual", "obj", "probe", "measured"] + TABLE_NAMES
LOAD_ORDER = ["views", "obj", "right", "left", "probe", "measured", "half", "dual"] + [
    "across", "along", "to_view", "to_line", "along16", "spread"
]


def kernel(tiles, count, *rest):
    far = dict(zip(LOADED, rest))
    rest = rest[len(LOADED) :]
    obj_out, views_out, dual_out, probe_out = rest[:4]
    rest = rest[4:]
    near = dict(zip(LOADED[1:], rest))
    (
        extended, grads, chunks, power, grad_out, grad_in, target, spec, lines, back, grid,
        came, now_send, now_came, after_send, after_came, chunks_came, slabs, gathered_rows,
        halo_sem, grad_sem, target_sem, now_sem, after_sem, chunk_sem, slab_sem, row_sem, load_sem,
    ) = rest[len(LOADED) - 1 :]
    obj, dual, probe, measured = (near[name] for name in ("obj", "dual", "probe", "measured"))
    t = near
    slab, ang = lax.axis_index("slab"), lax.axis_index("ang")

    def slab_peer(k):
        return lax.rem(slab + k, N_SLAB)

    across_x, across_y, core = ang // 8, lax.rem(ang // 2, 4), lax.rem(ang, 2)
    others = [
        lax.rem(across_x + x, 4) * 8 + lax.rem(across_y + y, 4) * 2 + lax.rem(core + c, 2) for x, y, c in OFFSETS
    ]

    def each_ang(body):
        for p in others:
            body(p)

    def remote(src, dst, sems, to):
        return pltpu.make_async_remote_copy(
            src_ref=src, dst_ref=dst, send_sem=sems.at[0], recv_sem=sems.at[1], device_id=to, device_id_type=MESH
        )

    def block(ref, p):
        return ref.at[:, pl.ds(pl.multiple_of(p * SLICE_DEV, SLICE_DEV), SLICE_DEV), :]

    def await_bytes(ref, sem):
        pltpu.make_async_copy(ref, ref, sem).wait()

    near["views"] = extended.at[:, :ROWS, :]
    loads = {}
    for name in LOAD_ORDER:
        loads[name] = pltpu.make_async_copy(far[name], near[name], load_sem.at[LOAD_ORDER.index(name)])
    barrier = pltpu.get_barrier_semaphore()
    each_ang(lambda p: pl.semaphore_signal(barrier, inc=1, device_id=(slab, p), device_id_type=MESH))
    for k in range(1, N_SLAB):
        pl.semaphore_signal(barrier, inc=1, device_id=(slab_peer(k), ang), device_id_type=MESH)
    for name in LOAD_ORDER:
        loads[name].start()
    pl.semaphore_wait(barrier, ANGLES - 1 + N_SLAB - 1)

    loads["views"].wait()
    halo_copy = remote(
        extended.at[:, :HALO, :], extended.at[:, ROWS:, :], halo_sem, (slab_peer(N_SLAB - 1), ang)
    )
    pl.when(slab > 0)(halo_copy.start)
    for name in ("obj", "right", "left"):
        loads[name].wait()
    spectrum(obj, t, spec)
    for name in ("probe", "measured", "half", "dual"):
        loads[name].wait()
    pl.when(slab < N_SLAB - 1)(halo_copy.wait_recv)

    @pl.when(slab == N_SLAB - 1)
    def _():
        extended[:, ROWS:, :] = jnp.zeros((2, HALO, SIDE), F32)

    picked = [tiles[0, n] for n in range(CAP)]
    starts = [tile * STEP for tile in picked]
    patches(extended, probe, measured, starts, count[0, 0], t, grads, chunks, power)
    each_ang(lambda p: remote(chunks.at[p], chunks_came.at[ang], chunk_sem, (slab, p)).start())
    chunks_came[ang] = chunks[ang]

    def gathered(r):
        sums = [None, None]
        for n in range(CAP):
            at = (lax.max(lax.min(r - picked[n], SIDE // STEP), -1) + 1) * STEP
            for c in range(2):
                piece = grads[n, c, pl.ds(at, STEP), :]
                sums[c] = piece if sums[c] is None else sums[c] + piece
        return sums

    def outer(r, carry):
        sums = gathered(r + ROWS // STEP)
        for c in range(2):
            grad_out[c, pl.ds(pl.multiple_of(r * STEP, STEP), STEP), :] = sums[c]
        return carry

    lax.fori_loop(0, HALO // STEP, outer, 0)
    grad_copy = remote(grad_out, grad_in, grad_sem, (slab_peer(1), ang))
    pl.when(slab < N_SLAB - 1)(grad_copy.start)

    def inside(r, carry):
        sums = gathered(r)
        at = pl.ds(pl.multiple_of(r * STEP, STEP), STEP)
        for c in range(2):
            target[c, at, :] = (1.0 - view_rate) * (extended[c, at, :] + dual[c, at, :]) - view_rate * sums[c]
        return carry

    lax.fori_loop(0, ROWS // STEP, inside, 0)

    def send_target(p):
        remote(block(target, p), came.at[ang], target_sem, (slab, p)).start()

    ready = HALO // SLICE_DEV
    each_ang(lambda p: pl.when(p >= ready)(lambda: send_target(p)))

    @pl.when(slab > 0)
    def _():
        grad_copy.wait_recv()
        target[:, :HALO, :] = target[:, :HALO, :] - view_rate * grad_in[...]

    each_ang(lambda p: pl.when(p < ready)(lambda: send_target(p)))
    came[ang] = target[:, pl.ds(pl.multiple_of(ang * SLICE_DEV, SLICE_DEV), SLICE_DEV), :]

    for name in ("across", "along", "to_view", "to_line", "along16", "spread"):
        loads[name].wait()

    def put_line(c, a, samples):
        lines[c, a] = samples

    def sample_now(c, carry):
        sample(spec, c, t, put_line)
        return carry

    lax.fori_loop(0, 2, sample_now, 0)

    def put_now(c, value):
        now_send[:, c] = value

    lines_to_views(lines, t, put_now)
    await_bytes(chunks_came.at[: ANGLES - 1], chunk_sem.at[1])
    slabs[slab, :8, :] = jnp.sum(chunks_came[...], axis=0)
    slabs[slab, 8:, :] = power[...]
    for k in range(1, N_SLAB):
        remote(slabs.at[slab], slabs.at[slab], slab_sem, (slab_peer(k), ang)).start()

    await_bytes(came.at[: ANGLES - 1], target_sem.at[1])
    each_ang(lambda p: remote(now_send.at[p], block(now_came, ang), now_sem, (slab, p)).start())
    now_came[:, pl.ds(pl.multiple_of(ang * SLICE_DEV, SLICE_DEV), SLICE_DEV), :] = now_send[ang]
    joined = jnp.concatenate([came[:, c].reshape(ROWS, SIDE) for c in range(2)], axis=1).astype(BF16)
    pulled = dot(joined, t["to_line"][...])
    for c in range(2):
        back[c] = (1.0 - view_rate) * lines[c] - pulled[:, c * SIDE : (c + 1) * SIDE].reshape(ANGLES, SLICE_DEV, SIDE)

    def put_after(c, a, samples):
        lines[c, a] = lines[c, a] - samples * (1.0 / ANGLES)

    def spread_back(c, carry):
        spread(back, c, t, grid)
        return carry

    def sample_after(c, carry):
        sample(grid, c, t, put_after)
        return carry

    lax.fori_loop(0, 2, spread_back, 0)
    await_bytes(slabs.at[: N_SLAB - 1], slab_sem.at[1])
    gathered_rows[ang] = jnp.sum(slabs[...], axis=0)
    each_ang(lambda p: remote(gathered_rows.at[ang], gathered_rows.at[ang], row_sem, (slab, p)).start())
    lax.fori_loop(0, 2, sample_after, 0)

    def put_views(c, value):
        after_send[:, c] = value

    lines_to_views(lines, t, put_views)
    each_ang(lambda p: remote(after_send.at[p], block(after_came, ang), after_sem, (slab, p)).start())
    after_came[:, pl.ds(pl.multiple_of(ang * SLICE_DEV, SLICE_DEV), SLICE_DEV), :] = after_send[ang]

    def put_object(c, z, value):
        obj_out[c, z] = obj[c, z] - value

    correction(grid, t, put_object)
    await_bytes(block_span(now_came), now_sem.at[1])
    views_out[...] = target[...] - dual[...] + view_rate * now_came[...]
    await_bytes(gathered_rows.at[: ANGLES - 1], row_sem.at[1])
    scale = probe_rate / (jnp.sum(gathered_rows[:, 8:, :]) * (1.0 / (SIDE * SIDE)) + epsilon)
    for c in range(2):
        rows = gathered_rows[c * 16 : (c + 1) * 16, :8, :].reshape(SIDE, SIDE)
        probe_out[c] = probe[c] - rows * scale
    await_bytes(block_span(after_came), after_sem.at[1])
    dual_out[...] = target[...] + view_rate * now_came[...] - after_came[...]

    await_bytes(came.at[: ANGLES - 1], target_sem.at[0])
    await_bytes(now_send.at[: ANGLES - 1], now_sem.at[0])
    await_bytes(after_send.at[: ANGLES - 1], after_sem.at[0])
    await_bytes(chunks_came.at[: ANGLES - 1], chunk_sem.at[0])
    await_bytes(slabs.at[: N_SLAB - 1], slab_sem.at[0])
    await_bytes(gathered_rows.at[: ANGLES - 1], row_sem.at[0])
    pl.when(slab > 0)(halo_copy.wait_send)
    pl.when(slab < N_SLAB - 1)(grad_copy.wait_send)


def store_all(*refs):
    copies = [pltpu.make_async_copy(refs[i], refs[4 + i], refs[8].at[i]) for i in range(4)]
    for copy in copies:
        copy.start()
    for copy in copies:
        copy.wait()


def block_span(ref):
    return ref.at[:, : SLICE_DEV * (ANGLES - 1), :]


def body(object_slices, views, scaled_dual, probe, intensities, tile_rows, live_counts):
    table = tables()
    arrays = dict(
        views=views.reshape(2, ROWS, SIDE),
        dual=scaled_dual.reshape(2, ROWS, SIDE),
        obj=object_slices,
        probe=probe,
        measured=intensities.reshape(CAP, SIDE, SIDE),
        **{name: jnp.asarray(table[name]) for name in TABLE_NAMES},
    )
    far, smem = pl.BlockSpec(memory_space=pltpu.HBM), pl.BlockSpec(memory_space=pltpu.SMEM)
    blocks = (ANGLES, 2, SLICE_DEV, SIDE)
    dma = pltpu.SemaphoreType.DMA((2,))
    scratch = [pltpu.VMEM(arrays[name].shape, arrays[name].dtype) for name in LOADED[1:]] + [
        pltpu.VMEM((2, ROWS + HALO, SIDE), F32),
        pltpu.VMEM((CAP, 2, SIDE + 2 * STEP, SIDE), F32),
        pltpu.VMEM((ANGLES, 8, SIDE), F32),
        pltpu.VMEM((8, SIDE), F32),
        pltpu.VMEM((2, HALO, SIDE), F32),
        pltpu.VMEM((2, HALO, SIDE), F32),
        pltpu.VMEM((2, ROWS, SIDE), F32),
        pltpu.VMEM((2, SLICE_DEV, SIDE, 2 * SIDE), BF16),
        pltpu.VMEM((2, ANGLES, SLICE_DEV, SIDE), F32),
        pltpu.VMEM((2, ANGLES, SLICE_DEV, SIDE), F32),
        pltpu.VMEM((2, SLICE_DEV, SIDE, SIDE), BF16),
        pltpu.VMEM(blocks, F32),
        pltpu.VMEM(blocks, F32),
        pltpu.VMEM((2, ROWS, SIDE), F32),
        pltpu.VMEM(blocks, F32),
        pltpu.VMEM((2, ROWS, SIDE), F32),
        pltpu.VMEM((ANGLES, 8, SIDE), F32),
        pltpu.VMEM((N_SLAB, 16, SIDE), F32),
        pltpu.VMEM((ANGLES, 16, SIDE), F32),
    ]
    near = pl.BlockSpec(memory_space=pltpu.VMEM)
    results = [
        jax.ShapeDtypeStruct(object_slices.shape, F32),
        jax.ShapeDtypeStruct((2, ROWS, SIDE), F32),
        jax.ShapeDtypeStruct((2, ROWS, SIDE), F32),
        jax.ShapeDtypeStruct(probe.shape, F32),
    ]
    made = pl.pallas_call(
        kernel,
        out_shape=results,
        in_specs=[smem] * 2 + [far] * len(LOADED),
        out_specs=[near] * 4,
        scratch_shapes=scratch
        + [dma] * 8
        + [pltpu.SemaphoreType.DMA((len(LOADED),))],
        compiler_params=pltpu.CompilerParams(collective_id=0, has_side_effects=True, vmem_limit_bytes=56 * 1024 * 1024),
    )(tile_rows, live_counts, *[arrays[name] for name in LOADED])
    obj_new, views_new, dual_new, probe_new = pl.pallas_call(
        store_all,
        out_shape=results,
        in_specs=[near] * 4,
        out_specs=[far] * 4,
        scratch_shapes=[pltpu.SemaphoreType.DMA((4,))],
    )(*made)
    return (
        obj_new,
        views_new.reshape(views.shape),
        dual_new.reshape(scaled_dual.shape),
        probe_new,
    )


def solution(mesh):
    in_specs = (
        P(None, ("slab", "ang"), None, None),
        P(None, "slab", "ang", None),
        P(None, "slab", "ang", None),
        P(),
        P("ang", "slab", None, None),
        P("ang", "slab"),
        P("ang", "slab"),
    )
    out_specs = (
        P(None, ("slab", "ang"), None, None),
        P(None, "slab", "ang", None),
        P(None, "slab", "ang", None),
        P(),
    )
    return jax.shard_map(body, mesh=mesh, in_specs=in_specs, out_specs=out_specs, check_vma=False)
```

```python
import math

import jax
import jax.numpy as jnp
import ml_dtypes
import numpy as np
from jax import lax
from jax.experimental import pallas as pl
from jax.experimental.pallas import tpu as pltpu
from jax.sharding import PartitionSpec as P

SIDE = 128
HALF = SIDE // 2
STEP = 16
ANGLES = 32
SLICE_DEV = 8
ROWS = ANGLES * SLICE_DEV
CAP = 12
BATCH = 4
HALO = SIDE - STEP
N_SLAB = 4
QUARTER = ANGLES // 2

view_rate = 0.1
probe_rate = 16.0
epsilon = 1e-06

F32 = jnp.float32
BF16 = jnp.bfloat16
MESH = pl.DeviceIdType.MESH

GROUPS = [(0, 1), (2, 3), (4, 5), (6, 7), (8, 9), (10, 11), (12, 13), (14, 15), (16,)]
OFFSETS = sorted(
    [(x, y, core) for x in range(4) for y in range(4) for core in range(2)][1:],
    key=lambda o: -(min(o[0], 4 - o[0]) + min(o[1], 4 - o[1])),
)
REACH = [16, 32, 32, 48, 64, 64, 64, 64, 64]

SAMPLE_BATCH = {16: 4, 32: 4, 48: 4, 64: 4}
SPREAD_BATCH = 4
EARLY, LATE = (8, 7, 5, 3, 1), (6, 4, 2, 0)


def dft_tables():
    counter = np.arange(SIDE)
    product = (counter[:, None] * counter[None, :] % SIDE).astype(np.float32)
    angle = product * np.float32(2.0 * math.pi / SIDE)
    factor = np.float32(1.0 / math.sqrt(SIDE))
    return (np.cos(angle) * factor).astype(np.float32), (np.sin(angle) * factor).astype(np.float32)


def split_table(table):
    high = table.astype(ml_dtypes.bfloat16)
    low = (table - high.astype(np.float32)).astype(ml_dtypes.bfloat16)
    return np.stack([high, low])


def hat(position):
    cells = np.arange(SIDE)[:, None] - HALF
    distance = np.abs(cells - position[None, :])
    return np.maximum(0.0, 1.0 - np.minimum(distance, SIDE - distance))


def tables():
    cosine, sine = dft_tables()
    shift_c, shift_s = np.roll(cosine, HALF, axis=0), np.roll(sine, HALF, axis=0)
    right = np.block([[shift_c.T, -shift_s.T], [shift_s.T, shift_c.T]])
    left = np.ascontiguousarray(right.T)
    sign = (1 - 2 * (np.arange(SIDE) % 2)).astype(np.float32)[None, :]
    to_view = np.block([[cosine * sign, sine * sign], [-sine * sign, cosine * sign]])
    half_left = np.block([[cosine, sine], [-sine, cosine]]).astype(ml_dtypes.bfloat16)
    half_right = np.block([[cosine, -sine], [sine, cosine]]).astype(ml_dtypes.bfloat16)
    radius = np.arange(SIDE) - HALF
    along = np.zeros((len(GROUPS), 2, SIDE, 2 * SIDE), np.float32)
    across = np.zeros((len(GROUPS), SIDE, 2 * SIDE), np.float32)
    for g, members in enumerate(GROUPS):
        for i, b in enumerate(members):
            lanes = slice(i * SIDE, (i + 1) * SIDE)
            row = radius * math.sin(math.pi * b / ANGLES)
            along[g, 0, :, lanes] = hat(row)
            if 0 < b < QUARTER:
                along[g, 1, :, lanes] = hat(-row)
            across[g, :, lanes] = hat(radius * math.cos(math.pi * b / ANGLES))
    return dict(
        right=split_table(right),
        left=split_table(left),
        to_view=split_table(to_view),
        to_line=np.ascontiguousarray(to_view.T).astype(ml_dtypes.bfloat16),
        half=np.stack([half_left, half_right]),
        along=along,
        along16=along.astype(ml_dtypes.bfloat16),
        across=np.concatenate([across, across], axis=1).astype(ml_dtypes.bfloat16),
        spread=np.ascontiguousarray(np.swapaxes(across, 1, 2)).astype(ml_dtypes.bfloat16),
    )


TABLE_NAMES = ["right", "left", "to_view", "to_line", "half", "along", "along16", "across", "spread"]


def dot(a, b):
    return jnp.dot(a, b, preferred_element_type=F32)


def split(x):
    high = x.astype(BF16)
    return high, (x - high.astype(F32)).astype(BF16)


def beside(x):
    return jnp.concatenate([x[: x.shape[0] // 2], x[x.shape[0] // 2 :]], axis=1)


def stacked(x):
    return jnp.concatenate([x[:, : x.shape[1] // 2], x[:, x.shape[1] // 2 :]], axis=0)


def spectrum(obj, t, out):
    for i in range(SLICE_DEV // 2):
        rows = [jnp.concatenate([obj[0, 2 * i + z], obj[1, 2 * i + z]], axis=1) for z in range(2)]
        high, low = split(jnp.concatenate(rows, axis=0))
        half = dot(high, t["right"][0]) + dot(low, t["right"][0]) + dot(high, t["right"][1])
        cols = jnp.concatenate([stacked(half[:SIDE]), stacked(half[SIDE:])], axis=1)
        high, low = split(cols)
        full = dot(t["left"][0], high) + dot(t["left"][0], low) + dot(t["left"][1], high)
        high, low = split(full)
        for z in range(2):
            for c in range(2):
                rows, lanes = slice(c * SIDE, (c + 1) * SIDE), slice(z * SIDE, (z + 1) * SIDE)
                out[c, 2 * i + z, :, :SIDE] = high[rows, lanes]
                out[c, 2 * i + z, :, SIDE:] = low[rows, lanes]


def sample(plane, c, t, put, groups):
    depth = plane.shape[-1]
    for g in groups:
        members = GROUPS[g]
        lanes = len(members) * SIDE
        low, top = HALF - REACH[g], HALF + REACH[g]
        batch = SAMPLE_BATCH[REACH[g]]
        sums = [[], []]
        for first in range(0, SLICE_DEV, batch):
            rows = plane[c, first : first + batch, low:top, :].reshape(batch * (top - low), depth)
            rows = dot(rows, t["across"][g, :depth, :lanes]).reshape(batch, top - low, lanes)
            for side in range(len(members)):
                weight = t["along"][g, side, low:top, :lanes]
                for z in range(batch):
                    sums[side].append(jnp.sum(rows[z] * weight, axis=0, keepdims=True))
        for side in range(len(members)):
            whole = jnp.concatenate(sums[side], axis=0)
            for i, b in enumerate(members):
                if side == 0 or b > 0:
                    put(c, QUARTER - b if side == 0 else QUARTER + b, whole[:, i * SIDE : (i + 1) * SIDE])


def spread(lines, c, t, out):
    for first in range(0, SLICE_DEV, SPREAD_BATCH):
        totals = [None] * SPREAD_BATCH
        for g, members in enumerate(GROUPS):
            lanes = len(members) * SIDE
            low, top = HALF - REACH[g], HALF + REACH[g]
            batch = []
            for z in range(first, first + SPREAD_BATCH):
                terms = None
                for side in range(len(members)):
                    picks = [lines[c, (QUARTER - b) if side == 0 else (QUARTER + b), z : z + 1, :] for b in members]
                    line = jnp.concatenate(picks, axis=1).astype(BF16)
                    term = t["along16"][g, side, low:top, :lanes] * line
                    terms = term if terms is None else terms + term
                batch.append(terms)
            parts = dot(jnp.concatenate(batch, axis=0), t["spread"][g, :lanes, :])
            for i in range(SPREAD_BATCH):
                part, total = parts[i * (top - low) : (i + 1) * (top - low)], totals[i]
                if total is not None:
                    edge = (part.shape[0] - total.shape[0]) // 2
                    inner = part[edge : edge + total.shape[0]] + total
                    part = jnp.concatenate([part[:edge], inner, part[edge + total.shape[0] :]], axis=0) if edge else inner
                totals[i] = part
        for i in range(SPREAD_BATCH):
            out[c, first + i] = totals[i].astype(BF16)


def angles_of(groups):
    members = [b for g in groups for b in GROUPS[g]]
    return sorted({QUARTER - b for b in members} | {QUARTER + b for b in members if b < QUARTER})


def is_early(p):
    below = (p < QUARTER) & (lax.rem((ANGLES + QUARTER - p) // 2, 2) == 1)
    above = (p >= QUARTER) & (lax.rem((p + QUARTER) // 2, 2) == 1)
    return below | above | (p == 0)


def lines_to_views(lines, t, angles, out):
    joined = jnp.concatenate([jnp.concatenate([lines[c, a] for a in angles], axis=0) for c in range(2)], axis=1)
    high, low = split(joined)
    result = dot(high, t["to_view"][0]) + dot(low, t["to_view"][0]) + dot(high, t["to_view"][1])
    for i, a in enumerate(angles):
        for c in range(2):
            out[a, c] = result[i * SLICE_DEV : (i + 1) * SLICE_DEV, c * SIDE : (c + 1) * SIDE]


def correction(grid, t, put):
    for i in range(SLICE_DEV // 2):
        rows = [jnp.concatenate([grid[0, 2 * i + z], grid[1, 2 * i + z]], axis=1) for z in range(2)]
        half = dot(jnp.concatenate(rows, axis=0), t["left"][0]).astype(BF16)
        cols = jnp.concatenate([stacked(half[:SIDE]), stacked(half[SIDE:])], axis=1)
        full = dot(t["right"][0], cols) * (1.0 / ANGLES)
        for z in range(2):
            for c in range(2):
                put(c, 2 * i + z, full[c * SIDE : (c + 1) * SIDE, z * SIDE : (z + 1) * SIDE])


def patches(extended, probe, measured, starts, count, t, grads, chunks, power):
    probe_re, probe_im = probe[0], probe[1]
    edge = jnp.zeros((2, STEP, SIDE), F32)
    for first in range(0, CAP, BATCH):
        slots = range(first, first + BATCH)
        exits = []
        for n in slots:
            re = extended[0, pl.ds(starts[n], SIDE), :]
            im = extended[1, pl.ds(starts[n], SIDE), :]
            exits.append(jnp.concatenate([probe_re * re - probe_im * im, probe_re * im + probe_im * re], axis=0).astype(BF16))
        half = dot(t["half"][0], jnp.concatenate(exits, axis=1)).astype(BF16)
        field = dot(
            jnp.concatenate([beside(half[:, i * SIDE : (i + 1) * SIDE]) for i in range(BATCH)], axis=0), t["half"][1]
        )
        pulls = []
        for i, n in enumerate(slots):
            field_re = field[i * SIDE : (i + 1) * SIDE, :SIDE]
            field_im = field[i * SIDE : (i + 1) * SIDE, SIDE:]
            live = jnp.where(n < count, 1.0, 0.0).astype(F32)
            misfit = (field_re * field_re + field_im * field_im - measured[n].astype(F32)) * live
            pulls.append(jnp.concatenate([field_re * misfit, field_im * misfit], axis=0).astype(BF16))
        half = dot(t["half"][1], jnp.concatenate(pulls, axis=1)).astype(BF16)
        back = dot(
            jnp.concatenate([beside(half[:, i * SIDE : (i + 1) * SIDE]) for i in range(BATCH)], axis=0), t["half"][0]
        )
        sum_re = sum_im = squares = None
        for i, n in enumerate(slots):
            re = extended[0, pl.ds(starts[n], SIDE), :]
            im = extended[1, pl.ds(starts[n], SIDE), :]
            live = jnp.where(n < count, 1.0, 0.0).astype(F32)
            back_re = back[i * SIDE : (i + 1) * SIDE, :SIDE]
            back_im = back[i * SIDE : (i + 1) * SIDE, SIDE:]
            grads[n, 0, STEP : STEP + SIDE, :] = probe_re * back_re + probe_im * back_im
            grads[n, 1, STEP : STEP + SIDE, :] = probe_re * back_im - probe_im * back_re
            grads[n, :, :STEP, :] = edge
            grads[n, :, STEP + SIDE :, :] = edge
            term_re = re * back_re + im * back_im
            term_im = re * back_im - im * back_re
            square = jnp.sum((re * re + im * im).reshape(SIDE // 8, 8, SIDE), axis=0) * live
            sum_re = term_re if sum_re is None else sum_re + term_re
            sum_im = term_im if sum_im is None else sum_im + term_im
            squares = square if squares is None else squares + square
        for i in range(ANGLES):
            part = (sum_re, sum_im)[i // 16][(i % 16) * 8 : (i % 16 + 1) * 8]
            chunks[i] = chunks[i] + part if first else part
        power[...] = power[...] + squares if first else squares


LOADED = ["views", "dual", "obj", "probe", "measured"] + TABLE_NAMES
LOAD_ORDER = ["views", "obj", "right", "left", "probe", "measured", "half", "dual"] + [
    "across", "along", "to_view", "to_line", "along16", "spread"
]


def kernel(tiles, count, *rest):
    far = dict(zip(LOADED, rest))
    rest = rest[len(LOADED) :]
    obj_out, views_out, dual_out, probe_out = rest[:4]
    rest = rest[4:]
    near = dict(zip(LOADED[1:], rest))
    (
        extended, grads, chunks, power, grad_out, grad_in, target, spec, lines, back, grid,
        came, now_send, now_came, after_send, after_came, chunks_came, slabs, gathered_rows,
        halo_sem, grad_sem, target_sem, now_sem, after_sem, chunk_sem, slab_sem, row_sem, load_sem,
    ) = rest[len(LOADED) - 1 :]
    obj, dual, probe, measured = (near[name] for name in ("obj", "dual", "probe", "measured"))
    t = near
    slab, ang = lax.axis_index("slab"), lax.axis_index("ang")

    def slab_peer(k):
        return lax.rem(slab + k, N_SLAB)

    across_x, across_y, core = ang // 8, lax.rem(ang // 2, 4), lax.rem(ang, 2)
    others = [
        lax.rem(across_x + x, 4) * 8 + lax.rem(across_y + y, 4) * 2 + lax.rem(core + c, 2) for x, y, c in OFFSETS
    ]

    def each_ang(body):
        for p in others:
            body(p)

    def remote(src, dst, sems, to):
        return pltpu.make_async_remote_copy(
            src_ref=src, dst_ref=dst, send_sem=sems.at[0], recv_sem=sems.at[1], device_id=to, device_id_type=MESH
        )

    def block(ref, p):
        return ref.at[:, pl.ds(pl.multiple_of(p * SLICE_DEV, SLICE_DEV), SLICE_DEV), :]

    def await_bytes(ref, sem):
        pltpu.make_async_copy(ref, ref, sem).wait()

    near["views"] = extended.at[:, :ROWS, :]
    loads = {}
    for name in LOAD_ORDER:
        loads[name] = pltpu.make_async_copy(far[name], near[name], load_sem.at[LOAD_ORDER.index(name)])
    barrier = pltpu.get_barrier_semaphore()
    each_ang(lambda p: pl.semaphore_signal(barrier, inc=1, device_id=(slab, p), device_id_type=MESH))
    for k in range(1, N_SLAB):
        pl.semaphore_signal(barrier, inc=1, device_id=(slab_peer(k), ang), device_id_type=MESH)
    for name in LOAD_ORDER:
        loads[name].start()
    pl.semaphore_wait(barrier, ANGLES - 1 + N_SLAB - 1)

    loads["views"].wait()
    halo_copy = remote(
        extended.at[:, :HALO, :], extended.at[:, ROWS:, :], halo_sem, (slab_peer(N_SLAB - 1), ang)
    )
    pl.when(slab > 0)(halo_copy.start)
    for name in ("obj", "right", "left"):
        loads[name].wait()
    spectrum(obj, t, spec)
    for name in ("probe", "measured", "half", "dual"):
        loads[name].wait()
    pl.when(slab < N_SLAB - 1)(halo_copy.wait_recv)

    @pl.when(slab == N_SLAB - 1)
    def _():
        extended[:, ROWS:, :] = jnp.zeros((2, HALO, SIDE), F32)

    picked = [tiles[0, n] for n in range(CAP)]
    starts = [tile * STEP for tile in picked]
    patches(extended, probe, measured, starts, count[0, 0], t, grads, chunks, power)
    each_ang(lambda p: remote(chunks.at[p], chunks_came.at[ang], chunk_sem, (slab, p)).start())
    chunks_came[ang] = chunks[ang]

    def gathered(r):
        sums = [None, None]
        for n in range(CAP):
            at = (lax.max(lax.min(r - picked[n], SIDE // STEP), -1) + 1) * STEP
            for c in range(2):
                piece = grads[n, c, pl.ds(at, STEP), :]
                sums[c] = piece if sums[c] is None else sums[c] + piece
        return sums

    def outer(r, carry):
        sums = gathered(r + ROWS // STEP)
        for c in range(2):
            grad_out[c, pl.ds(pl.multiple_of(r * STEP, STEP), STEP), :] = sums[c]
        return carry

    lax.fori_loop(0, HALO // STEP, outer, 0)
    grad_copy = remote(grad_out, grad_in, grad_sem, (slab_peer(1), ang))
    pl.when(slab < N_SLAB - 1)(grad_copy.start)

    def inside(r, carry):
        sums = gathered(r)
        at = pl.ds(pl.multiple_of(r * STEP, STEP), STEP)
        for c in range(2):
            target[c, at, :] = (1.0 - view_rate) * (extended[c, at, :] + dual[c, at, :]) - view_rate * sums[c]
        return carry

    lax.fori_loop(0, ROWS // STEP, inside, 0)

    def send_target(p):
        remote(block(target, p), came.at[ang], target_sem, (slab, p)).start()

    ready = HALO // SLICE_DEV
    each_ang(lambda p: pl.when(p >= ready)(lambda: send_target(p)))

    @pl.when(slab > 0)
    def _():
        grad_copy.wait_recv()
        target[:, :HALO, :] = target[:, :HALO, :] - view_rate * grad_in[...]

    each_ang(lambda p: pl.when(p < ready)(lambda: send_target(p)))
    came[ang] = target[:, pl.ds(pl.multiple_of(ang * SLICE_DEV, SLICE_DEV), SLICE_DEV), :]

    for name in ("across", "along", "to_view", "to_line", "along16", "spread"):
        loads[name].wait()

    def put_line(c, a, samples):
        lines[c, a] = samples

    def sample_now(groups):
        def plane(c, carry):
            sample(spec, c, t, put_line, groups)
            return carry

        lax.fori_loop(0, 2, plane, 0)

    sample_now(EARLY)
    await_bytes(chunks_came.at[: ANGLES - 1], chunk_sem.at[1])
    slabs[slab, :8, :] = jnp.sum(chunks_came[...], axis=0)
    slabs[slab, 8:, :] = power[...]
    for k in range(1, N_SLAB):
        remote(slabs.at[slab], slabs.at[slab], slab_sem, (slab_peer(k), ang)).start()
    sample_now(LATE)
    lines_to_views(lines, t, range(ANGLES), now_send)

    await_bytes(came.at[: ANGLES - 1], target_sem.at[1])
    each_ang(lambda p: remote(now_send.at[p], block(now_came, ang), now_sem, (slab, p)).start())
    now_came[:, pl.ds(pl.multiple_of(ang * SLICE_DEV, SLICE_DEV), SLICE_DEV), :] = now_send[ang]
    joined = jnp.concatenate([came[:, c].reshape(ROWS, SIDE) for c in range(2)], axis=1).astype(BF16)
    pulled = dot(joined, t["to_line"][...])
    for c in range(2):
        back[c] = (1.0 - view_rate) * lines[c] - pulled[:, c * SIDE : (c + 1) * SIDE].reshape(ANGLES, SLICE_DEV, SIDE)

    def put_after(c, a, samples):
        lines[c, a] = lines[c, a] - samples * (1.0 / ANGLES)

    def spread_back(c, carry):
        spread(back, c, t, grid)
        return carry

    def sample_after(groups):
        def plane(c, carry):
            sample(grid, c, t, put_after, groups)
            return carry

        lax.fori_loop(0, 2, plane, 0)
        lines_to_views(lines, t, angles_of(groups), after_send)

    def send_after(p):
        remote(after_send.at[p], block(after_came, ang), after_sem, (slab, p)).start()

    lax.fori_loop(0, 2, spread_back, 0)
    await_bytes(slabs.at[: N_SLAB - 1], slab_sem.at[1])
    gathered_rows[ang] = jnp.sum(slabs[...], axis=0)
    each_ang(lambda p: remote(gathered_rows.at[ang], gathered_rows.at[ang], row_sem, (slab, p)).start())
    sample_after(EARLY)
    each_ang(lambda p: pl.when(is_early(p))(lambda: send_after(p)))
    sample_after(LATE)
    each_ang(lambda p: pl.when(jnp.logical_not(is_early(p)))(lambda: send_after(p)))
    after_came[:, pl.ds(pl.multiple_of(ang * SLICE_DEV, SLICE_DEV), SLICE_DEV), :] = after_send[ang]

    def put_object(c, z, value):
        obj_out[c, z] = obj[c, z] - value

    correction(grid, t, put_object)
    await_bytes(block_span(now_came), now_sem.at[1])
    views_out[...] = target[...] - dual[...] + view_rate * now_came[...]
    await_bytes(gathered_rows.at[: ANGLES - 1], row_sem.at[1])
    scale = probe_rate / (jnp.sum(gathered_rows[:, 8:, :]) * (1.0 / (SIDE * SIDE)) + epsilon)
    for c in range(2):
        rows = gathered_rows[c * 16 : (c + 1) * 16, :8, :].reshape(SIDE, SIDE)
        probe_out[c] = probe[c] - rows * scale
    await_bytes(block_span(after_came), after_sem.at[1])
    dual_out[...] = target[...] + view_rate * now_came[...] - after_came[...]

    await_bytes(came.at[: ANGLES - 1], target_sem.at[0])
    await_bytes(now_send.at[: ANGLES - 1], now_sem.at[0])
    await_bytes(after_send.at[: ANGLES - 1], after_sem.at[0])
    await_bytes(chunks_came.at[: ANGLES - 1], chunk_sem.at[0])
    await_bytes(slabs.at[: N_SLAB - 1], slab_sem.at[0])
    await_bytes(gathered_rows.at[: ANGLES - 1], row_sem.at[0])
    pl.when(slab > 0)(halo_copy.wait_send)
    pl.when(slab < N_SLAB - 1)(grad_copy.wait_send)


def store_all(*refs):
    copies = [pltpu.make_async_copy(refs[i], refs[4 + i], refs[8].at[i]) for i in range(4)]
    for copy in copies:
        copy.start()
    for copy in copies:
        copy.wait()


def block_span(ref):
    return ref.at[:, : SLICE_DEV * (ANGLES - 1), :]


def body(object_slices, views, scaled_dual, probe, intensities, tile_rows, live_counts):
    table = tables()
    arrays = dict(
        views=views.reshape(2, ROWS, SIDE),
        dual=scaled_dual.reshape(2, ROWS, SIDE),
        obj=object_slices,
        probe=probe,
        measured=intensities.reshape(CAP, SIDE, SIDE),
        **{name: jnp.asarray(table[name]) for name in TABLE_NAMES},
    )
    far, smem = pl.BlockSpec(memory_space=pltpu.HBM), pl.BlockSpec(memory_space=pltpu.SMEM)
    blocks = (ANGLES, 2, SLICE_DEV, SIDE)
    dma = pltpu.SemaphoreType.DMA((2,))
    scratch = [pltpu.VMEM(arrays[name].shape, arrays[name].dtype) for name in LOADED[1:]] + [
        pltpu.VMEM((2, ROWS + HALO, SIDE), F32),
        pltpu.VMEM((CAP, 2, SIDE + 2 * STEP, SIDE), F32),
        pltpu.VMEM((ANGLES, 8, SIDE), F32),
        pltpu.VMEM((8, SIDE), F32),
        pltpu.VMEM((2, HALO, SIDE), F32),
        pltpu.VMEM((2, HALO, SIDE), F32),
        pltpu.VMEM((2, ROWS, SIDE), F32),
        pltpu.VMEM((2, SLICE_DEV, SIDE, 2 * SIDE), BF16),
        pltpu.VMEM((2, ANGLES, SLICE_DEV, SIDE), F32),
        pltpu.VMEM((2, ANGLES, SLICE_DEV, SIDE), F32),
        pltpu.VMEM((2, SLICE_DEV, SIDE, SIDE), BF16),
        pltpu.VMEM(blocks, F32),
        pltpu.VMEM(blocks, F32),
        pltpu.VMEM((2, ROWS, SIDE), F32),
        pltpu.VMEM(blocks, F32),
        pltpu.VMEM((2, ROWS, SIDE), F32),
        pltpu.VMEM((ANGLES, 8, SIDE), F32),
        pltpu.VMEM((N_SLAB, 16, SIDE), F32),
        pltpu.VMEM((ANGLES, 16, SIDE), F32),
    ]
    near = pl.BlockSpec(memory_space=pltpu.VMEM)
    results = [
        jax.ShapeDtypeStruct(object_slices.shape, F32),
        jax.ShapeDtypeStruct((2, ROWS, SIDE), F32),
        jax.ShapeDtypeStruct((2, ROWS, SIDE), F32),
        jax.ShapeDtypeStruct(probe.shape, F32),
    ]
    made = pl.pallas_call(
        kernel,
        out_shape=results,
        in_specs=[smem] * 2 + [far] * len(LOADED),
        out_specs=[near] * 4,
        scratch_shapes=scratch
        + [dma] * 8
        + [pltpu.SemaphoreType.DMA((len(LOADED),))],
        compiler_params=pltpu.CompilerParams(collective_id=0, has_side_effects=True, vmem_limit_bytes=56 * 1024 * 1024),
    )(tile_rows, live_counts, *[arrays[name] for name in LOADED])
    obj_new, views_new, dual_new, probe_new = pl.pallas_call(
        store_all,
        out_shape=results,
        in_specs=[near] * 4,
        out_specs=[far] * 4,
        scratch_shapes=[pltpu.SemaphoreType.DMA((4,))],
    )(*made)
    return (
        obj_new,
        views_new.reshape(views.shape),
        dual_new.reshape(scaled_dual.shape),
        probe_new,
    )


def solution(mesh):
    in_specs = (
        P(None, ("slab", "ang"), None, None),
        P(None, "slab", "ang", None),
        P(None, "slab", "ang", None),
        P(),
        P("ang", "slab", None, None),
        P("ang", "slab"),
        P("ang", "slab"),
    )
    out_specs = (
        P(None, ("slab", "ang"), None, None),
        P(None, "slab", "ang", None),
        P(None, "slab", "ang", None),
        P(),
    )
    return jax.shard_map(body, mesh=mesh, in_specs=in_specs, out_specs=out_specs, check_vma=False)
```

```python
import math

import jax
import jax.numpy as jnp
import ml_dtypes
import numpy as np
from jax import lax
from jax.experimental import pallas as pl
from jax.experimental.pallas import tpu as pltpu
from jax.sharding import PartitionSpec as P

SIDE = 128
HALF = SIDE // 2
STEP = 16
ANGLES = 32
SLICE_DEV = 8
ROWS = ANGLES * SLICE_DEV
CAP = 12
BATCH = 6
HALO = SIDE - STEP
N_SLAB = 4
QUARTER = ANGLES // 2

view_rate = 0.1
probe_rate = 16.0
epsilon = 1e-06

F32 = jnp.float32
BF16 = jnp.bfloat16
MESH = pl.DeviceIdType.MESH

GROUPS = [(0, 1), (2, 3), (4, 5), (6, 7), (8, 9), (10, 11), (12, 13), (14, 15), (16,)]
OFFSETS = sorted(
    [(x, y, core) for x in range(4) for y in range(4) for core in range(2)][1:],
    key=lambda o: -(min(o[0], 4 - o[0]) + min(o[1], 4 - o[1])),
)
REACH = [16, 32, 32, 48, 64, 64, 64, 64, 64]

SAMPLE_BATCH = {16: 4, 32: 4, 48: 4, 64: 4}
SPREAD_BATCH = 4
EARLY, LATE = (8, 7, 6, 5, 3, 1), (4, 2, 0)


def dft_tables():
    counter = np.arange(SIDE)
    product = (counter[:, None] * counter[None, :] % SIDE).astype(np.float32)
    angle = product * np.float32(2.0 * math.pi / SIDE)
    factor = np.float32(1.0 / math.sqrt(SIDE))
    return (np.cos(angle) * factor).astype(np.float32), (np.sin(angle) * factor).astype(np.float32)


def split_table(table):
    high = table.astype(ml_dtypes.bfloat16)
    low = (table - high.astype(np.float32)).astype(ml_dtypes.bfloat16)
    return np.stack([high, low])


def hat(position):
    cells = np.arange(SIDE)[:, None] - HALF
    distance = np.abs(cells - position[None, :])
    return np.maximum(0.0, 1.0 - np.minimum(distance, SIDE - distance))


def tables():
    cosine, sine = dft_tables()
    shift_c, shift_s = np.roll(cosine, HALF, axis=0), np.roll(sine, HALF, axis=0)
    right = np.block([[shift_c.T, -shift_s.T], [shift_s.T, shift_c.T]])
    left = np.ascontiguousarray(right.T)
    sign = (1 - 2 * (np.arange(SIDE) % 2)).astype(np.float32)[None, :]
    to_view = np.block([[cosine * sign, sine * sign], [-sine * sign, cosine * sign]])
    half_left = np.block([[cosine, sine], [-sine, cosine]]).astype(ml_dtypes.bfloat16)
    half_right = np.block([[cosine, -sine], [sine, cosine]]).astype(ml_dtypes.bfloat16)
    radius = np.arange(SIDE) - HALF
    along = np.zeros((len(GROUPS), 2, SIDE, 2 * SIDE), np.float32)
    across = np.zeros((len(GROUPS), SIDE, 2 * SIDE), np.float32)
    for g, members in enumerate(GROUPS):
        for i, b in enumerate(members):
            lanes = slice(i * SIDE, (i + 1) * SIDE)
            row = radius * math.sin(math.pi * b / ANGLES)
            along[g, 0, :, lanes] = hat(row)
            if 0 < b < QUARTER:
                along[g, 1, :, lanes] = hat(-row)
            across[g, :, lanes] = hat(radius * math.cos(math.pi * b / ANGLES))
    return dict(
        right=split_table(right),
        left=split_table(left),
        to_view=split_table(to_view),
        to_line=np.ascontiguousarray(to_view.T).astype(ml_dtypes.bfloat16),
        half=np.stack([half_left, half_right]),
        along=along,
        along16=along.astype(ml_dtypes.bfloat16),
        across=np.concatenate([across, across], axis=1).astype(ml_dtypes.bfloat16),
        spread=np.ascontiguousarray(np.swapaxes(across, 1, 2)).astype(ml_dtypes.bfloat16),
    )


TABLE_NAMES = ["right", "left", "to_view", "to_line", "half", "along", "along16", "across", "spread"]


def dot(a, b):
    return jnp.dot(a, b, preferred_element_type=F32)


def split(x):
    high = x.astype(BF16)
    return high, (x - high.astype(F32)).astype(BF16)


def beside(x):
    return jnp.concatenate([x[: x.shape[0] // 2], x[x.shape[0] // 2 :]], axis=1)


def stacked(x):
    return jnp.concatenate([x[:, : x.shape[1] // 2], x[:, x.shape[1] // 2 :]], axis=0)


def spectrum(obj, t, out):
    for i in range(SLICE_DEV // 2):
        rows = [jnp.concatenate([obj[0, 2 * i + z], obj[1, 2 * i + z]], axis=1) for z in range(2)]
        high, low = split(jnp.concatenate(rows, axis=0))
        half = dot(high, t["right"][0]) + dot(low, t["right"][0]) + dot(high, t["right"][1])
        cols = jnp.concatenate([stacked(half[:SIDE]), stacked(half[SIDE:])], axis=1)
        high, low = split(cols)
        full = dot(t["left"][0], high) + dot(t["left"][0], low) + dot(t["left"][1], high)
        high, low = split(full)
        for z in range(2):
            for c in range(2):
                rows, lanes = slice(c * SIDE, (c + 1) * SIDE), slice(z * SIDE, (z + 1) * SIDE)
                out[c, 2 * i + z, :, :SIDE] = high[rows, lanes]
                out[c, 2 * i + z, :, SIDE:] = low[rows, lanes]


def sample(plane, c, t, put, groups):
    depth = plane.shape[-1]
    for g in groups:
        members = GROUPS[g]
        lanes = len(members) * SIDE
        low, top = HALF - REACH[g], HALF + REACH[g]
        batch = SAMPLE_BATCH[REACH[g]]
        sums = [[], []]
        for first in range(0, SLICE_DEV, batch):
            rows = plane[c, first : first + batch, low:top, :].reshape(batch * (top - low), depth)
            rows = dot(rows, t["across"][g, :depth, :lanes]).reshape(batch, top - low, lanes)
            for side in range(len(members)):
                weight = t["along"][g, side, low:top, :lanes]
                for z in range(batch):
                    sums[side].append(jnp.sum(rows[z] * weight, axis=0, keepdims=True))
        for side in range(len(members)):
            whole = jnp.concatenate(sums[side], axis=0)
            for i, b in enumerate(members):
                if side == 0 or b > 0:
                    put(c, QUARTER - b if side == 0 else QUARTER + b, whole[:, i * SIDE : (i + 1) * SIDE])


def spread(lines, c, t, out):
    for first in range(0, SLICE_DEV, SPREAD_BATCH):
        totals = [None] * SPREAD_BATCH
        for g, members in enumerate(GROUPS):
            lanes = len(members) * SIDE
            low, top = HALF - REACH[g], HALF + REACH[g]
            batch = []
            for z in range(first, first + SPREAD_BATCH):
                terms = None
                for side in range(len(members)):
                    picks = [lines[c, (QUARTER - b) if side == 0 else (QUARTER + b), z : z + 1, :] for b in members]
                    line = jnp.concatenate(picks, axis=1).astype(BF16)
                    term = t["along16"][g, side, low:top, :lanes] * line
                    terms = term if terms is None else terms + term
                batch.append(terms)
            parts = dot(jnp.concatenate(batch, axis=0), t["spread"][g, :lanes, :])
            for i in range(SPREAD_BATCH):
                part, total = parts[i * (top - low) : (i + 1) * (top - low)], totals[i]
                if total is not None:
                    edge = (part.shape[0] - total.shape[0]) // 2
                    inner = part[edge : edge + total.shape[0]] + total
                    part = jnp.concatenate([part[:edge], inner, part[edge + total.shape[0] :]], axis=0) if edge else inner
                totals[i] = part
        for i in range(SPREAD_BATCH):
            out[c, first + i] = totals[i].astype(BF16)


def angles_of(groups):
    members = [b for g in groups for b in GROUPS[g]]
    return sorted({QUARTER - b for b in members} | {QUARTER + b for b in members if b < QUARTER})


def is_early(p):
    below = (p < QUARTER) & (lax.rem((ANGLES + QUARTER - p) // 2, 2) == 1)
    above = (p >= QUARTER) & (lax.rem((p + QUARTER) // 2, 2) == 1)
    return below | above | (p <= 4) | (p >= 28)


def lines_to_views(lines, t, angles, out):
    joined = jnp.concatenate([jnp.concatenate([lines[c, a] for a in angles], axis=0) for c in range(2)], axis=1)
    high, low = split(joined)
    result = dot(high, t["to_view"][0]) + dot(low, t["to_view"][0]) + dot(high, t["to_view"][1])
    for i, a in enumerate(angles):
        for c in range(2):
            out[a, c] = result[i * SLICE_DEV : (i + 1) * SLICE_DEV, c * SIDE : (c + 1) * SIDE]


def correction(grid, t, put):
    for i in range(SLICE_DEV // 2):
        rows = [jnp.concatenate([grid[0, 2 * i + z], grid[1, 2 * i + z]], axis=1) for z in range(2)]
        half = dot(jnp.concatenate(rows, axis=0), t["left"][0]).astype(BF16)
        cols = jnp.concatenate([stacked(half[:SIDE]), stacked(half[SIDE:])], axis=1)
        full = dot(t["right"][0], cols) * (1.0 / ANGLES)
        for z in range(2):
            for c in range(2):
                put(c, 2 * i + z, full[c * SIDE : (c + 1) * SIDE, z * SIDE : (z + 1) * SIDE])


def patches(extended, probe, measured, starts, count, t, grads, chunks, power):
    probe_re, probe_im = probe[0], probe[1]
    edge = jnp.zeros((2, STEP, SIDE), F32)
    for first in range(0, CAP, BATCH):
        slots = range(first, first + BATCH)
        exits = []
        for n in slots:
            re = extended[0, pl.ds(starts[n], SIDE), :]
            im = extended[1, pl.ds(starts[n], SIDE), :]
            exits.append(jnp.concatenate([probe_re * re - probe_im * im, probe_re * im + probe_im * re], axis=0).astype(BF16))
        half = dot(t["half"][0], jnp.concatenate(exits, axis=1)).astype(BF16)
        field = dot(
            jnp.concatenate([beside(half[:, i * SIDE : (i + 1) * SIDE]) for i in range(BATCH)], axis=0), t["half"][1]
        )
        pulls = []
        for i, n in enumerate(slots):
            field_re = field[i * SIDE : (i + 1) * SIDE, :SIDE]
            field_im = field[i * SIDE : (i + 1) * SIDE, SIDE:]
            live = jnp.where(n < count, 1.0, 0.0).astype(F32)
            misfit = (field_re * field_re + field_im * field_im - measured[n].astype(F32)) * live
            pulls.append(jnp.concatenate([field_re * misfit, field_im * misfit], axis=0).astype(BF16))
        half = dot(t["half"][1], jnp.concatenate(pulls, axis=1)).astype(BF16)
        back = dot(
            jnp.concatenate([beside(half[:, i * SIDE : (i + 1) * SIDE]) for i in range(BATCH)], axis=0), t["half"][0]
        )
        sum_re = sum_im = squares = None
        for i, n in enumerate(slots):
            re = extended[0, pl.ds(starts[n], SIDE), :]
            im = extended[1, pl.ds(starts[n], SIDE), :]
            live = jnp.where(n < count, 1.0, 0.0).astype(F32)
            back_re = back[i * SIDE : (i + 1) * SIDE, :SIDE]
            back_im = back[i * SIDE : (i + 1) * SIDE, SIDE:]
            grads[n, 0, STEP : STEP + SIDE, :] = probe_re * back_re + probe_im * back_im
            grads[n, 1, STEP : STEP + SIDE, :] = probe_re * back_im - probe_im * back_re
            grads[n, :, :STEP, :] = edge
            grads[n, :, STEP + SIDE :, :] = edge
            term_re = re * back_re + im * back_im
            term_im = re * back_im - im * back_re
            square = jnp.sum((re * re + im * im).reshape(SIDE // 8, 8, SIDE), axis=0) * live
            sum_re = term_re if sum_re is None else sum_re + term_re
            sum_im = term_im if sum_im is None else sum_im + term_im
            squares = square if squares is None else squares + square
        for i in range(ANGLES):
            part = (sum_re, sum_im)[i // 16][(i % 16) * 8 : (i % 16 + 1) * 8]
            chunks[i] = chunks[i] + part if first else part
        power[...] = power[...] + squares if first else squares


LOADED = ["views", "dual", "obj", "probe", "measured"] + TABLE_NAMES
LOAD_ORDER = ["views", "obj", "right", "left", "probe", "measured", "half", "dual"] + [
    "across", "along", "to_view", "to_line", "along16", "spread"
]


def kernel(tiles, count, *rest):
    far = dict(zip(LOADED, rest))
    rest = rest[len(LOADED) :]
    obj_out, views_out, dual_out, probe_out = rest[:4]
    rest = rest[4:]
    near = dict(zip(LOADED[1:], rest))
    (
        extended, grads, chunks, power, grad_out, grad_in, target, spec, lines, back, grid,
        came, now_send, now_came, after_send, after_came, chunks_came, slabs, gathered_rows,
        halo_sem, grad_sem, target_sem, now_sem, after_sem, chunk_sem, slab_sem, row_sem, load_sem,
    ) = rest[len(LOADED) - 1 :]
    obj, dual, probe, measured = (near[name] for name in ("obj", "dual", "probe", "measured"))
    t = near
    slab, ang = lax.axis_index("slab"), lax.axis_index("ang")

    def slab_peer(k):
        return lax.rem(slab + k, N_SLAB)

    across_x, across_y, core = ang // 8, lax.rem(ang // 2, 4), lax.rem(ang, 2)
    others = [
        lax.rem(across_x + x, 4) * 8 + lax.rem(across_y + y, 4) * 2 + lax.rem(core + c, 2) for x, y, c in OFFSETS
    ]

    def each_ang(body):
        for p in others:
            body(p)

    def remote(src, dst, sems, to):
        return pltpu.make_async_remote_copy(
            src_ref=src, dst_ref=dst, send_sem=sems.at[0], recv_sem=sems.at[1], device_id=to, device_id_type=MESH
        )

    def block(ref, p):
        return ref.at[:, pl.ds(pl.multiple_of(p * SLICE_DEV, SLICE_DEV), SLICE_DEV), :]

    def await_bytes(ref, sem):
        pltpu.make_async_copy(ref, ref, sem).wait()

    near["views"] = extended.at[:, :ROWS, :]
    loads = {}
    for name in LOAD_ORDER:
        loads[name] = pltpu.make_async_copy(far[name], near[name], load_sem.at[LOAD_ORDER.index(name)])
    barrier = pltpu.get_barrier_semaphore()
    each_ang(lambda p: pl.semaphore_signal(barrier, inc=1, device_id=(slab, p), device_id_type=MESH))
    for k in range(1, N_SLAB):
        pl.semaphore_signal(barrier, inc=1, device_id=(slab_peer(k), ang), device_id_type=MESH)
    for name in LOAD_ORDER:
        loads[name].start()
    pl.semaphore_wait(barrier, ANGLES - 1 + N_SLAB - 1)

    loads["views"].wait()
    halo_copy = remote(
        extended.at[:, :HALO, :], extended.at[:, ROWS:, :], halo_sem, (slab_peer(N_SLAB - 1), ang)
    )
    pl.when(slab > 0)(halo_copy.start)
    for name in ("obj", "right", "left"):
        loads[name].wait()
    spectrum(obj, t, spec)
    for name in ("probe", "measured", "half", "dual"):
        loads[name].wait()
    pl.when(slab < N_SLAB - 1)(halo_copy.wait_recv)

    @pl.when(slab == N_SLAB - 1)
    def _():
        extended[:, ROWS:, :] = jnp.zeros((2, HALO, SIDE), F32)

    picked = [tiles[0, n] for n in range(CAP)]
    starts = [tile * STEP for tile in picked]
    patches(extended, probe, measured, starts, count[0, 0], t, grads, chunks, power)
    each_ang(lambda p: remote(chunks.at[p], chunks_came.at[ang], chunk_sem, (slab, p)).start())
    chunks_came[ang] = chunks[ang]

    def gathered(r):
        sums = [None, None]
        for n in range(CAP):
            at = (lax.max(lax.min(r - picked[n], SIDE // STEP), -1) + 1) * STEP
            for c in range(2):
                piece = grads[n, c, pl.ds(at, STEP), :]
                sums[c] = piece if sums[c] is None else sums[c] + piece
        return sums

    def outer(r, carry):
        sums = gathered(r + ROWS // STEP)
        for c in range(2):
            grad_out[c, pl.ds(pl.multiple_of(r * STEP, STEP), STEP), :] = sums[c]
        return carry

    lax.fori_loop(0, HALO // STEP, outer, 0)
    grad_copy = remote(grad_out, grad_in, grad_sem, (slab_peer(1), ang))
    pl.when(slab < N_SLAB - 1)(grad_copy.start)

    def inside(r, carry):
        sums = gathered(r)
        at = pl.ds(pl.multiple_of(r * STEP, STEP), STEP)
        for c in range(2):
            target[c, at, :] = (1.0 - view_rate) * (extended[c, at, :] + dual[c, at, :]) - view_rate * sums[c]
        return carry

    lax.fori_loop(0, ROWS // STEP, inside, 0)

    def send_target(p):
        remote(block(target, p), came.at[ang], target_sem, (slab, p)).start()

    ready = HALO // SLICE_DEV
    each_ang(lambda p: pl.when(p >= ready)(lambda: send_target(p)))

    @pl.when(slab > 0)
    def _():
        grad_copy.wait_recv()
        target[:, :HALO, :] = target[:, :HALO, :] - view_rate * grad_in[...]

    each_ang(lambda p: pl.when(p < ready)(lambda: send_target(p)))
    came[ang] = target[:, pl.ds(pl.multiple_of(ang * SLICE_DEV, SLICE_DEV), SLICE_DEV), :]

    for name in ("across", "along", "to_view", "to_line", "along16", "spread"):
        loads[name].wait()

    def put_line(c, a, samples):
        lines[c, a] = samples

    def sample_now(groups):
        def plane(c, carry):
            sample(spec, c, t, put_line, groups)
            return carry

        lax.fori_loop(0, 2, plane, 0)

    sample_now(EARLY)
    await_bytes(chunks_came.at[: ANGLES - 1], chunk_sem.at[1])
    slabs[slab, :8, :] = jnp.sum(chunks_came[...], axis=0)
    slabs[slab, 8:, :] = power[...]
    for k in range(1, N_SLAB):
        remote(slabs.at[slab], slabs.at[slab], slab_sem, (slab_peer(k), ang)).start()
    sample_now(LATE)
    lines_to_views(lines, t, range(ANGLES), now_send)

    each_ang(lambda p: remote(now_send.at[p], block(now_came, ang), now_sem, (slab, p)).start())
    now_came[:, pl.ds(pl.multiple_of(ang * SLICE_DEV, SLICE_DEV), SLICE_DEV), :] = now_send[ang]
    await_bytes(came.at[: ANGLES - 1], target_sem.at[1])
    joined = jnp.concatenate([came[:, c].reshape(ROWS, SIDE) for c in range(2)], axis=1).astype(BF16)
    pulled = dot(joined, t["to_line"][...])
    for c in range(2):
        back[c] = (1.0 - view_rate) * lines[c] - pulled[:, c * SIDE : (c + 1) * SIDE].reshape(ANGLES, SLICE_DEV, SIDE)

    def put_after(c, a, samples):
        lines[c, a] = lines[c, a] - samples * (1.0 / ANGLES)

    def spread_back(c, carry):
        spread(back, c, t, grid)
        return carry

    def sample_after(groups):
        def plane(c, carry):
            sample(grid, c, t, put_after, groups)
            return carry

        lax.fori_loop(0, 2, plane, 0)
        lines_to_views(lines, t, angles_of(groups), after_send)

    def send_after(p):
        remote(after_send.at[p], block(after_came, ang), after_sem, (slab, p)).start()

    lax.fori_loop(0, 2, spread_back, 0)
    await_bytes(slabs.at[: N_SLAB - 1], slab_sem.at[1])
    gathered_rows[ang] = jnp.sum(slabs[...], axis=0)
    each_ang(lambda p: remote(gathered_rows.at[ang], gathered_rows.at[ang], row_sem, (slab, p)).start())
    sample_after(EARLY)
    each_ang(lambda p: pl.when(is_early(p))(lambda: send_after(p)))
    sample_after(LATE)
    each_ang(lambda p: pl.when(jnp.logical_not(is_early(p)))(lambda: send_after(p)))
    after_came[:, pl.ds(pl.multiple_of(ang * SLICE_DEV, SLICE_DEV), SLICE_DEV), :] = after_send[ang]

    def put_object(c, z, value):
        obj_out[c, z] = obj[c, z] - value

    correction(grid, t, put_object)
    await_bytes(block_span(now_came), now_sem.at[1])
    views_out[...] = target[...] - dual[...] + view_rate * now_came[...]
    await_bytes(gathered_rows.at[: ANGLES - 1], row_sem.at[1])
    scale = probe_rate / (jnp.sum(gathered_rows[:, 8:, :]) * (1.0 / (SIDE * SIDE)) + epsilon)
    for c in range(2):
        rows = gathered_rows[c * 16 : (c + 1) * 16, :8, :].reshape(SIDE, SIDE)
        probe_out[c] = probe[c] - rows * scale
    await_bytes(block_span(after_came), after_sem.at[1])
    dual_out[...] = target[...] + view_rate * now_came[...] - after_came[...]

    await_bytes(came.at[: ANGLES - 1], target_sem.at[0])
    await_bytes(now_send.at[: ANGLES - 1], now_sem.at[0])
    await_bytes(after_send.at[: ANGLES - 1], after_sem.at[0])
    await_bytes(chunks_came.at[: ANGLES - 1], chunk_sem.at[0])
    await_bytes(slabs.at[: N_SLAB - 1], slab_sem.at[0])
    await_bytes(gathered_rows.at[: ANGLES - 1], row_sem.at[0])
    pl.when(slab > 0)(halo_copy.wait_send)
    pl.when(slab < N_SLAB - 1)(grad_copy.wait_send)


def store_all(*refs):
    copies = [pltpu.make_async_copy(refs[i], refs[4 + i], refs[8].at[i]) for i in range(4)]
    for copy in copies:
        copy.start()
    for copy in copies:
        copy.wait()


def block_span(ref):
    return ref.at[:, : SLICE_DEV * (ANGLES - 1), :]


def body(object_slices, views, scaled_dual, probe, intensities, tile_rows, live_counts):
    table = tables()
    arrays = dict(
        views=views.reshape(2, ROWS, SIDE),
        dual=scaled_dual.reshape(2, ROWS, SIDE),
        obj=object_slices,
        probe=probe,
        measured=intensities.reshape(CAP, SIDE, SIDE),
        **{name: jnp.asarray(table[name]) for name in TABLE_NAMES},
    )
    far, smem = pl.BlockSpec(memory_space=pltpu.HBM), pl.BlockSpec(memory_space=pltpu.SMEM)
    blocks = (ANGLES, 2, SLICE_DEV, SIDE)
    dma = pltpu.SemaphoreType.DMA((2,))
    scratch = [pltpu.VMEM(arrays[name].shape, arrays[name].dtype) for name in LOADED[1:]] + [
        pltpu.VMEM((2, ROWS + HALO, SIDE), F32),
        pltpu.VMEM((CAP, 2, SIDE + 2 * STEP, SIDE), F32),
        pltpu.VMEM((ANGLES, 8, SIDE), F32),
        pltpu.VMEM((8, SIDE), F32),
        pltpu.VMEM((2, HALO, SIDE), F32),
        pltpu.VMEM((2, HALO, SIDE), F32),
        pltpu.VMEM((2, ROWS, SIDE), F32),
        pltpu.VMEM((2, SLICE_DEV, SIDE, 2 * SIDE), BF16),
        pltpu.VMEM((2, ANGLES, SLICE_DEV, SIDE), F32),
        pltpu.VMEM((2, ANGLES, SLICE_DEV, SIDE), F32),
        pltpu.VMEM((2, SLICE_DEV, SIDE, SIDE), BF16),
        pltpu.VMEM(blocks, F32),
        pltpu.VMEM(blocks, F32),
        pltpu.VMEM((2, ROWS, SIDE), F32),
        pltpu.VMEM(blocks, F32),
        pltpu.VMEM((2, ROWS, SIDE), F32),
        pltpu.VMEM((ANGLES, 8, SIDE), F32),
        pltpu.VMEM((N_SLAB, 16, SIDE), F32),
        pltpu.VMEM((ANGLES, 16, SIDE), F32),
    ]
    near = pl.BlockSpec(memory_space=pltpu.VMEM)
    results = [
        jax.ShapeDtypeStruct(object_slices.shape, F32),
        jax.ShapeDtypeStruct((2, ROWS, SIDE), F32),
        jax.ShapeDtypeStruct((2, ROWS, SIDE), F32),
        jax.ShapeDtypeStruct(probe.shape, F32),
    ]
    made = pl.pallas_call(
        kernel,
        out_shape=results,
        in_specs=[smem] * 2 + [far] * len(LOADED),
        out_specs=[near] * 4,
        scratch_shapes=scratch
        + [dma] * 8
        + [pltpu.SemaphoreType.DMA((len(LOADED),))],
        compiler_params=pltpu.CompilerParams(collective_id=0, has_side_effects=True, vmem_limit_bytes=56 * 1024 * 1024),
    )(tile_rows, live_counts, *[arrays[name] for name in LOADED])
    obj_new, views_new, dual_new, probe_new = pl.pallas_call(
        store_all,
        out_shape=results,
        in_specs=[near] * 4,
        out_specs=[far] * 4,
        scratch_shapes=[pltpu.SemaphoreType.DMA((4,))],
    )(*made)
    return (
        obj_new,
        views_new.reshape(views.shape),
        dual_new.reshape(scaled_dual.shape),
        probe_new,
    )


def solution(mesh):
    in_specs = (
        P(None, ("slab", "ang"), None, None),
        P(None, "slab", "ang", None),
        P(None, "slab", "ang", None),
        P(),
        P("ang", "slab", None, None),
        P("ang", "slab"),
        P("ang", "slab"),
    )
    out_specs = (
        P(None, ("slab", "ang"), None, None),
        P(None, "slab", "ang", None),
        P(None, "slab", "ang", None),
        P(),
    )
    return jax.shard_map(body, mesh=mesh, in_specs=in_specs, out_specs=out_specs, check_vma=False)
```
